128 devices in a mesh: frame: 8 (over x, y_lo), patch: 16 (over z, y_hi, core).
Axes of the slice: x: 4, y: 4 (y_hi: 2, y_lo: 2; y = y_hi * 2 + y_lo), z: 4, core: 2. Of those that a mesh axis runs over, the one named last changes fastest.
Arguments:
- tokens: bfloat16 [48, 768, 1152], P('frame', 'patch'), may hold values from -40 to 40
- cotangent: bfloat16 [48, 768, 1152], P('frame', 'patch'), may hold values from -6 to 6
- space_query: bfloat16 [1152, 1152], replicated, may hold values from -0.1875 to 0.1875
- space_key: bfloat16 [1152, 1152], replicated, may hold values from -0.1875 to 0.1875
- space_value: bfloat16 [1152, 1152], replicated, may hold values from -0.1875 to 0.1875
- space_out: bfloat16 [1152, 1152], replicated, may hold values from -0.75 to 0.75
- time_query: bfloat16 [1152, 1152], replicated, may hold values from -0.1875 to 0.1875
- time_key: bfloat16 [1152, 1152], replicated, may hold values from -0.1875 to 0.1875
- time_value: bfloat16 [1152, 1152], replicated, may hold values from -0.1875 to 0.1875
- time_out: bfloat16 [1152, 1152], replicated, may hold values from -0.75 to 0.75
Outputs:
- block_output: bfloat16 [48, 768, 1152], P('frame', 'patch')
- token_grad: bfloat16 [48, 768, 1152], P('frame', 'patch')
The draws below stay inside these ranges and needn't reach their ends.
All inputs are finite; a program needn't handle non-finite values.
Results may differ from the reference program's by a relative error of at most 0.035.
Values may be sent and summed in bfloat16 or wider, within the bound.
No kernel may reach another device: no remote copies, remote signals or barrier semaphores. Data moves between devices by JAX's collectives and lax.ppermute only.
A program may use at most 192 MiB of HBM per device.

```python
import math
import jax
import jax.numpy as jnp
from jax import lax

D = 1152
HEADS = 16
FRAMES = 48
PATCHES = 768


def draw_tokens(key, part):
    key = jax.random.fold_in(key, 7)
    base_key, row_key, col_key = jax.random.split(key, 3)
    row_scale = jnp.exp(jax.random.uniform(row_key, (FRAMES, PATCHES, 1), jnp.float32, math.log(0.3), math.log(3.0)))
    col_scale = jnp.exp(jax.random.uniform(col_key, (D,), jnp.float32, math.log(0.3), math.log(3.0)))
    base_draw = jnp.clip(jax.random.normal(base_key, (FRAMES, PATCHES, D), jnp.float32), -4.0, 4.0)
    result = row_scale * col_scale * base_draw
    return result.astype(jnp.bfloat16)


def shard_levels(stream_key, dims, cuts, low, high):
    gain = 1.0
    for dim, parts in cuts:
        draws = jax.random.uniform(jax.random.fold_in(jax.random.fold_in(stream_key, 6), dim), (parts,), jnp.float32, low / len(cuts), high / len(cuts))
        gain = gain * jnp.repeat(jnp.exp(draws), dims[dim] // parts).reshape((-1,) + (1,) * (len(dims) - 1 - dim))
    return gain


def gaussian(key, extent, deviation, bound, cuts=(), dtype=jnp.bfloat16):
    values = jax.random.normal(key, extent, jnp.float32) * deviation
    if len(cuts) > 0:
        values = shard_levels(key, extent, cuts, -0.22, 0.18) * values
    return jnp.clip(values, min=-bound, max=bound).astype(dtype)


def setup_inputs(seed: int = 0) -> dict:
    streams_of = jax.random.split(jax.random.key(seed), 11)
    return {
        "tokens": draw_tokens(jax.random.fold_in(streams_of[10], 71), 0),
        "cotangent": gaussian(streams_of[1], (FRAMES, PATCHES, D), 1.0, 6.0, ((0, 8), (1, 16))),
        "space_query": gaussian(streams_of[2], (D, D), D ** -0.5, 0.1875),
        "space_key": gaussian(streams_of[3], (D, D), D ** -0.5, 0.1875),
        "space_value": gaussian(streams_of[4], (D, D), D ** -0.5, 0.1875),
        "space_out": gaussian(streams_of[5], (D, D), (D // 16) ** -0.5, 0.75),
        "time_query": gaussian(streams_of[6], (D, D), D ** -0.5, 0.1875),
        "time_key": gaussian(streams_of[7], (D, D), D ** -0.5, 0.1875),
        "time_value": gaussian(streams_of[8], (D, D), D ** -0.5, 0.1875),
        "time_out": gaussian(streams_of[9], (D, D), (D // 16) ** -0.5, 0.75),
    }


eps = 1e-06

def project(normed, matrix):
    flat_rows = normed.reshape(-1, normed.shape[-1])
    result = jnp.dot(flat_rows, matrix, preferred_element_type=jnp.float32)
    return result.reshape(normed.shape[:-1] + (matrix.shape[1],))

def head_norm(projected):
    head_dim = D // HEADS
    pieces = projected.reshape(projected.shape[:-1] + (projected.shape[-1] // head_dim, head_dim))
    factor = lax.rsqrt(lax.optimization_barrier(jnp.mean(pieces * pieces, axis=-1, keepdims=True)) + eps)
    return (pieces * factor).astype(jnp.bfloat16).reshape(projected.shape)

def prepare(values, w_query, w_key, w_value):
    center = values - lax.optimization_barrier(jnp.mean(values, axis=-1, keepdims=True))
    normed = (center * lax.rsqrt(lax.optimization_barrier(jnp.mean(center * center, axis=-1, keepdims=True)) + eps)).astype(jnp.bfloat16)
    query = head_norm(project(normed, w_query))
    keys = head_norm(project(normed, w_key))
    value_rows = project(normed, w_value).astype(jnp.bfloat16)
    return (query, keys, value_rows)

def attention_core(query, keys, value_rows, time_first):
    head_dim = D // HEADS
    head_shape = query.shape[:-1] + (query.shape[-1] // head_dim, head_dim)
    query_heads = lax.optimization_barrier(query).reshape(head_shape).astype(jnp.float32)
    key_heads = lax.optimization_barrier(keys).reshape(head_shape).astype(jnp.float32)
    value_heads = lax.optimization_barrier(value_rows).reshape(head_shape).astype(jnp.float32)
    if time_first:
        scores = jnp.einsum('lbhe,mbhe->bhlm', query_heads, key_heads)
    else:
        scores = jnp.einsum('blhe,bmhe->bhlm', query_heads, key_heads)
    raised = jnp.exp(scores * (1.0 / math.sqrt(head_dim)))
    weights = (raised / lax.optimization_barrier(jnp.sum(raised, axis=-1, keepdims=True))).astype(jnp.bfloat16)
    weights = lax.optimization_barrier(weights).astype(jnp.float32)
    if time_first:
        mixed = jnp.einsum('bhlm,mbhe->lbhe', weights, value_heads)
    else:
        mixed = jnp.einsum('bhlm,bmhe->blhe', weights, value_heads)
    return mixed.reshape(query.shape).astype(jnp.bfloat16)

def finish(values, mixed, w_out):
    return (values + project(mixed, w_out)).astype(jnp.bfloat16)

def attend(tokens, weight_set, time_first):
    values = tokens.astype(jnp.float32)
    query, keys, value_rows = prepare(values, weight_set[0], weight_set[1], weight_set[2])
    return finish(values, attention_core(query, keys, value_rows, time_first), weight_set[3])

def reference(tokens, cotangent, space_query, space_key, space_value, space_out, time_query, time_key, time_value, time_out):
    space_set = (space_query, space_key, space_value, space_out)
    time_set = (time_query, time_key, time_value, time_out)

    def per_frame(frame_rows):
        return attend(frame_rows[None], space_set, False)[0]

    def per_column(column_rows):
        return attend(column_rows[:, None, :], time_set, True)[:, 0, :]

    def forward(inputs):
        spaced = lax.map(jax.checkpoint(per_frame), inputs)
        columns = jnp.swapaxes(spaced, 0, 1)
        timed = lax.map(jax.checkpoint(per_column), columns)
        return jnp.swapaxes(timed, 0, 1)
    block_output, pullback = jax.vjp(forward, tokens)
    token_grad, = pullback(cotangent)
    return (block_output, token_grad)
```

```python
import functools
import math

import jax
import jax.numpy as jnp
import numpy as np
from jax import lax
from jax.experimental import pallas as pl
from jax.experimental.pallas import tpu as pltpu
from jax.sharding import Mesh
from jax.sharding import PartitionSpec as P

D = 1152
HEADS = 16
HD = D // HEADS
WIN = 256
EPS = 1e-6
SCALE = 1.0 / math.sqrt(HD)
F32 = jnp.float32
BF16 = jnp.bfloat16
VMEM_LIMIT = 56 * 1024 * 1024

NN = (((1,), (0,)), ((), ()))
NT = (((1,), (1,)), ((), ()))
TN = (((0,), (0,)), ((), ()))


def dot(a, b, dims=NN):
    return lax.dot_general(a, b, dims, preferred_element_type=F32)


def head_sum_matrix():
    i = lax.broadcasted_iota(jnp.int32, (D, 128), 0)
    j = lax.broadcasted_iota(jnp.int32, (D, 128), 1) * HD
    return jnp.where((i >= j) & (i < j + HD), 1.0, 0.0).astype(BF16)


def head_spread_matrix():
    j = (lax.broadcasted_iota(jnp.int32, (256, D), 0) & 127) * HD
    i = lax.broadcasted_iota(jnp.int32, (256, D), 1)
    return jnp.where((i >= j) & (i < j + HD), 1.0, 0.0).astype(BF16)


def spread(r, spread_m):
    high = r.astype(BF16)
    low = (r - high.astype(F32)).astype(BF16)
    return dot(jnp.concatenate([high, low], axis=1), spread_m)


def layer_stats(x):
    mean = jnp.mean(x, axis=-1, keepdims=True)
    center = x - mean
    rstd = lax.rsqrt(jnp.mean(center * center, axis=-1, keepdims=True) + EPS)
    return center * rstd, rstd


def head_norm(z, sum_m, spread_m):
    s = dot((z * z).astype(BF16), sum_m)
    r = lax.rsqrt(s * (1.0 / HD) + EPS)
    return (z * spread(r, spread_m)).astype(BF16), r


def head_norm_back(dy, y, r, sum_m, spread_m):
    yf = y.astype(F32)
    m = dot((dy * yf).astype(BF16), sum_m) * (1.0 / HD)
    return (dy * spread(r, spread_m) - yf * spread(r * m, spread_m)).astype(BF16)


def layer_back(dy, normed, rstd):
    a = jnp.mean(dy, axis=-1, keepdims=True)
    b = jnp.mean(dy * normed, axis=-1, keepdims=True)
    return rstd * (dy - a - normed * b)


def head_window(h):
    start = jnp.minimum((h * HD) // 128 * 128, D - WIN)
    start = pl.multiple_of(start, 128)
    lane = lax.broadcasted_iota(jnp.int32, (1, WIN), 1) + start
    keep = (lane >= h * HD) & (lane < h * HD + HD)
    return pl.ds(start, WIN), keep


def call(body, out_shape, scratch, flops, nbytes, name):
    return pl.pallas_call(
        body,
        out_shape=out_shape,
        scratch_shapes=scratch,
        compiler_params=pltpu.CompilerParams(vmem_limit_bytes=VMEM_LIMIT),
        cost_estimate=pl.CostEstimate(flops=flops, bytes_accessed=nbytes, transcendentals=0),
        name=name,
    )


def sds(shape, dtype=BF16):
    return jax.ShapeDtypeStruct(shape, dtype)


def kv_body(x_ref, wk_ref, wv_ref, kv_ref, rk_ref):
    normed = layer_stats(x_ref[...].astype(F32))[0].astype(BF16)
    sum_m, spread_m = head_sum_matrix(), head_spread_matrix()
    k, rk = head_norm(dot(normed, wk_ref[...]), sum_m, spread_m)
    kv_ref[0] = k
    rk_ref[...] = rk
    kv_ref[1] = dot(normed, wv_ref[...]).astype(BF16)


def q_body(x_ref, wq_ref, q_ref, rq_ref):
    normed = layer_stats(x_ref[...].astype(F32))[0].astype(BF16)
    q, rq = head_norm(dot(normed, wq_ref[...]), head_sum_matrix(), head_spread_matrix())
    q_ref[...] = q
    rq_ref[...] = rq


def space_body(x_ref, q_ref, kv_ref, kvo_ref, wo_ref, out_ref, mixed_ref):
    def step(h, carry):
        win, keep = head_window(h)
        qm = jnp.where(keep, q_ref[:, win], 0.0).astype(BF16)
        total, out = 0.0, 0.0
        for ref in (kv_ref, kvo_ref):
            s = dot(qm, ref[0, :, win], NT)
            e = jnp.exp(s * SCALE)
            total = total + jnp.sum(e, axis=-1, keepdims=True)
            out = out + dot(e.astype(BF16), ref[1, :, win])
        out = out * (1.0 / total)
        mixed_ref[:, win] = jnp.where(keep, out, mixed_ref[:, win])
        return carry

    lax.fori_loop(0, HEADS, step, 0)
    out = x_ref[...].astype(F32) + dot(mixed_ref[...].astype(BF16), wo_ref[...])
    out_ref[...] = out.astype(BF16)


def back_body(g_ref, q_ref, kv_ref, kvo_ref, wo_ref, dq_ref, dkv_ref, dkvo_ref, do_ref, aq_ref, akv_ref):
    n = g_ref.shape[0]
    do_ref[...] = dot(g_ref[...], wo_ref[...], NT).astype(BF16)
    akv_ref[...] = jnp.zeros_like(akv_ref)

    def step(h, carry):
        win, keep = head_window(h)
        qm = jnp.where(keep, q_ref[:, win], 0.0).astype(BF16)
        dom = jnp.where(keep, do_ref[:, win], 0.0).astype(BF16)
        es, total = [], 0.0
        for ref in (kv_ref, kvo_ref):
            e = jnp.exp(dot(ref[0, :, win], qm, NT) * SCALE)
            total = total + jnp.sum(e, axis=0, keepdims=True)
            es.append(e)
        inv = 1.0 / total
        ps, dps, delta = [], [], 0.0
        for i, ref in enumerate((kv_ref, kvo_ref)):
            p = es[i] * inv
            dp = dot(ref[1, :, win], dom, NT)
            delta = delta + jnp.sum(p * dp, axis=0, keepdims=True)
            akv_ref[1, i, :, win] += dot(p.astype(BF16), dom)
            ps.append(p)
            dps.append(dp)
        dq = 0.0
        for i, ref in enumerate((kv_ref, kvo_ref)):
            ds = (ps[i] * (dps[i] - delta) * SCALE).astype(BF16)
            akv_ref[0, i, :, win] += dot(ds, qm)
            dq = dq + dot(ds, ref[0, :, win], TN)
        aq_ref[:, win] = jnp.where(keep, dq, aq_ref[:, win])
        return carry

    lax.fori_loop(0, HEADS, step, 0)
    dq_ref[...] = aq_ref[...].astype(BF16)
    for i in range(2):
        dkv_ref[i] = akv_ref[i, 0].astype(BF16)
        dkvo_ref[i] = akv_ref[i, 1].astype(BF16)


def final_body(x_ref, g_ref, q_ref, kv_ref, rq_ref, rk_ref, dq_ref, dkv_ref, got_ref, wq_ref, wk_ref, wv_ref, out_ref):
    sum_m, spread_m = head_sum_matrix(), head_spread_matrix()
    dq = head_norm_back(dq_ref[...].astype(F32), q_ref[...], rq_ref[...], sum_m, spread_m)
    grad = dot(dq, wq_ref[...], NT)
    dk = dkv_ref[0].astype(F32) + got_ref[0].astype(F32)
    dk = head_norm_back(dk, kv_ref[0], rk_ref[...], sum_m, spread_m)
    grad = grad + dot(dk, wk_ref[...], NT)
    dv = (dkv_ref[1].astype(F32) + got_ref[1].astype(F32)).astype(BF16)
    grad = grad + dot(dv, wv_ref[...], NT)
    normed, rstd = layer_stats(x_ref[...].astype(F32))
    out_ref[...] = (g_ref[...].astype(F32) + layer_back(grad, normed, rstd)).astype(BF16)


def time_body(
    x_ref, cot_ref, perm_ref, permt_ref, wq_ref, wk_ref, wv_ref, wo_ref,
    out_ref, grad_ref,
    q_ref, k_ref, v_ref, do_ref, mixed_ref, aq_ref, ak_ref, av_ref, mask_ref, g_ref,
):
    n = q_ref.shape[0]
    sum_m, spread_m = head_sum_matrix(), head_spread_matrix()
    normed = layer_stats(x_ref[pl.ds(0, n), :].astype(F32))[0].astype(BF16)
    q, rq = head_norm(dot(normed, wq_ref[...]), sum_m, spread_m)
    q_ref[...] = q
    k, rk = head_norm(dot(normed, wk_ref[...]), sum_m, spread_m)
    k_ref[...] = k
    v_ref[...] = dot(normed, wv_ref[...]).astype(BF16)
    g_ref[...] = dot(permt_ref[...], cot_ref[...]).astype(BF16)
    do_ref[...] = dot(g_ref[...], wo_ref[...], NT).astype(BF16)
    ak_ref[...] = jnp.zeros_like(ak_ref)
    av_ref[...] = jnp.zeros_like(av_ref)
    apart = lax.broadcasted_iota(jnp.int32, (n, n), 0) - lax.broadcasted_iota(jnp.int32, (n, n), 1)
    mask_ref[...] = jnp.where(lax.rem(apart, 6) == 0, 1.0, 0.0)

    def step(h, carry):
        win, keep = head_window(h)
        qm = jnp.where(keep, q_ref[:, win], 0.0).astype(BF16)
        dom = jnp.where(keep, do_ref[:, win], 0.0).astype(BF16)
        k, v = k_ref[:, win], v_ref[:, win]
        e = jnp.exp(dot(k, qm, NT) * SCALE) * mask_ref[...]
        p = e * (1.0 / jnp.sum(e, axis=0, keepdims=True))
        dp = dot(v, dom, NT)
        delta = jnp.sum(p * dp, axis=0, keepdims=True)
        pb = p.astype(BF16)
        ds = (p * (dp - delta) * SCALE).astype(BF16)
        mixed_ref[:, win] = jnp.where(keep, dot(pb, v, TN), mixed_ref[:, win])
        av_ref[:, win] += dot(pb, dom)
        ak_ref[:, win] += dot(ds, qm)
        aq_ref[:, win] = jnp.where(keep, dot(ds, k, TN), aq_ref[:, win])
        return carry

    lax.fori_loop(0, HEADS, step, 0)
    x = x_ref[pl.ds(0, n), :].astype(F32)
    out = (x + dot(mixed_ref[...].astype(BF16), wo_ref[...])).astype(BF16)
    out_ref[...] = dot(perm_ref[...], out).astype(BF16)
    dq = head_norm_back(aq_ref[...], q_ref[...], rq, sum_m, spread_m)
    grad = dot(dq, wq_ref[...], NT)
    dk = head_norm_back(ak_ref[...], k_ref[...], rk, sum_m, spread_m)
    grad = grad + dot(dk, wk_ref[...], NT)
    grad = grad + dot(av_ref[...].astype(BF16), wv_ref[...], NT)
    normed, rstd = layer_stats(x)
    grad_ref[pl.ds(0, n), :] = (g_ref[...].astype(F32) + layer_back(grad, normed, rstd)).astype(BF16)
    grad_ref[pl.ds(n, grad_ref.shape[0] - n), :] = jnp.zeros((grad_ref.shape[0] - n, D), BF16)


def perm_body(m_ref, a_ref, out_ref):
    out_ref[...] = dot(m_ref[...], a_ref[...]).astype(BF16)


def frame_permutation():
    m = np.zeros((320, 288), np.float32)
    for f in range(8):
        for c in range(6):
            for j in range(6):
                m[f * 40 + c * 6 + j, c * 48 + f * 6 + j] = 1.0
    return m


def local(tokens, cotangent, sq, sk, sv, so, tq, tk, tv, to):
    n, t = 384, 288
    swap = [(0, 1), (1, 0)]
    proj = 2 * n * D * D
    wb = 2 * D * D
    perm_np = frame_permutation()
    perm = jnp.asarray(perm_np, BF16)
    permt = jnp.asarray(np.ascontiguousarray(perm_np.T), BF16)

    x = jnp.pad(tokens, ((0, 2), (0, 0), (0, 0)))
    x = lax.all_to_all(x, "chip", 0, 0, tiled=True).reshape(n, D)

    cot = call(perm_body, sds((320, D)), [], 2 * 320 * t * D, 4 * t * D, "cot_pack")(
        perm, cotangent.reshape(t, D)
    )
    cot = lax.all_to_all(cot.reshape(8, 40, D), "frame", 0, 0, tiled=True).reshape(320, D)

    kv, rk = call(kv_body, (sds((2, n, D)), sds((n, 128), F32)), [], 2 * proj, 2 * wb, "space_kv")(x, sk, sv)
    kvo = lax.ppermute(kv, "core", swap)
    q, rq = call(q_body, (sds((n, D)), sds((n, 128), F32)), [], proj, wb, "space_q")(x, sq)
    spaced = call(space_body, sds((n, D)), [pltpu.VMEM((n, D), F32)], 12 * proj, 2 * wb, "space_mix")(
        x, q, kv, kvo, so
    )

    tx = lax.all_to_all(spaced.reshape(64, 2, 3 * D), ("chip", "frame"), 0, 0, tiled=True).reshape(n, D)
    tout, tgrad = call(
        time_body,
        (sds((320, D)), sds((n, D))),
        [pltpu.VMEM((t, D), BF16)] * 4 + [pltpu.VMEM((t, D), F32)] * 4 + [pltpu.VMEM((t, t), F32), pltpu.VMEM((t, D), BF16)],
        20 * proj,
        4 * wb,
        "time",
    )(tx, cot, perm, permt, tq, tk, tv, to)
    g = lax.all_to_all(tgrad.reshape(64, 2, 3 * D), ("chip", "frame"), 0, 0, tiled=True).reshape(n, D)
    tout = lax.all_to_all(tout.reshape(8, 40, D), "frame", 0, 0, tiled=True).reshape(320, D)
    block = call(perm_body, sds((t, D)), [], 2 * 320 * t * D, 4 * t * D, "out_unpack")(permt, tout)

    dq, dkv, dkvo = call(
        back_body,
        (sds((n, D)), sds((2, n, D)), sds((2, n, D))),
        [pltpu.VMEM((n, D), BF16), pltpu.VMEM((n, D), F32), pltpu.VMEM((2, 2, n, D), F32)],
        20 * proj,
        2 * wb,
        "space_back",
    )(g, q, kv, kvo, so)
    got = lax.ppermute(dkvo, "core", swap)
    grad = call(final_body, sds((n, D)), [], 3 * proj, 4 * wb, "space_final")(
        x, g, q, kv, rq, rk, dq, dkv, got, sq, sk, sv
    )
    grad = lax.all_to_all(grad.reshape(8, 48, D), "chip", 0, 0, tiled=True)[:6]
    return block.reshape(6, 48, D), grad


def solution(mesh):
    planes = Mesh(mesh.devices.reshape(8, 8, 2), ("frame", "chip", "core"))
    spec = P("frame", ("chip", "core"), None)
    return jax.shard_map(
        local,
        mesh=planes,
        in_specs=(spec, spec) + (P(),) * 8,
        out_specs=(spec, spec),
        check_vma=False,
    )
```

```python
import functools
import math

import jax
import jax.numpy as jnp
import numpy as np
from jax import lax
from jax.experimental import pallas as pl
from jax.experimental.pallas import tpu as pltpu
from jax.sharding import Mesh
from jax.sharding import PartitionSpec as P

D = 1152
HEADS = 16
HD = D // HEADS
WIN = 256
EPS = 1e-6
SCALE = 1.0 / math.sqrt(HD)
F32 = jnp.float32
BF16 = jnp.bfloat16
VMEM_LIMIT = 32 * 1024 * 1024

NN = (((1,), (0,)), ((), ()))
NT = (((1,), (1,)), ((), ()))
TN = (((0,), (0,)), ((), ()))


def dot(a, b, dims=NN):
    return lax.dot_general(a, b, dims, preferred_element_type=F32)


def head_sum_matrix():
    i = lax.broadcasted_iota(jnp.int32, (D, 128), 0)
    j = lax.broadcasted_iota(jnp.int32, (D, 128), 1) * HD
    return jnp.where((i >= j) & (i < j + HD), 1.0, 0.0).astype(BF16)


def head_spread_matrix():
    j = (lax.broadcasted_iota(jnp.int32, (256, D), 0) & 127) * HD
    i = lax.broadcasted_iota(jnp.int32, (256, D), 1)
    return jnp.where((i >= j) & (i < j + HD), 1.0, 0.0).astype(BF16)


def spread(r, spread_m):
    high = r.astype(BF16)
    low = (r - high.astype(F32)).astype(BF16)
    return dot(jnp.concatenate([high, low], axis=1), spread_m)


def layer_stats(x):
    mean = jnp.mean(x, axis=-1, keepdims=True)
    center = x - mean
    rstd = lax.rsqrt(jnp.mean(center * center, axis=-1, keepdims=True) + EPS)
    return center * rstd, rstd


def head_norm(z, sum_m, spread_m):
    s = dot((z * z).astype(BF16), sum_m)
    r = lax.rsqrt(s * (1.0 / HD) + EPS)
    return (z * spread(r, spread_m)).astype(BF16), r


def head_norm_back(dy, y, r, sum_m, spread_m):
    yf = y.astype(F32)
    m = dot((dy * yf).astype(BF16), sum_m) * (1.0 / HD)
    return (dy * spread(r, spread_m) - yf * spread(r * m, spread_m)).astype(BF16)


def layer_back(dy, normed, rstd):
    a = jnp.mean(dy, axis=-1, keepdims=True)
    b = jnp.mean(dy * normed, axis=-1, keepdims=True)
    return rstd * (dy - a - normed * b)


def head_window(h):
    start = min((h * HD) // 128 * 128, D - WIN)
    lane = lax.broadcasted_iota(jnp.int32, (1, WIN), 1) + start
    keep = (lane >= h * HD) & (lane < h * HD + HD)
    return pl.ds(start, WIN), keep


def call(body, out_shape, scratch, flops, nbytes, name):
    return pl.pallas_call(
        body,
        out_shape=out_shape,
        scratch_shapes=scratch,
        compiler_params=pltpu.CompilerParams(vmem_limit_bytes=VMEM_LIMIT),
        cost_estimate=pl.CostEstimate(flops=flops, bytes_accessed=nbytes, transcendentals=0),
        name=name,
    )


def sds(shape, dtype=BF16):
    return jax.ShapeDtypeStruct(shape, dtype)


def kv_body(x_ref, wk_ref, wv_ref, kv_ref, rk_ref):
    normed = layer_stats(x_ref[...].astype(F32))[0].astype(BF16)
    sum_m, spread_m = head_sum_matrix(), head_spread_matrix()
    k, rk = head_norm(dot(normed, wk_ref[...]), sum_m, spread_m)
    kv_ref[0] = k
    rk_ref[...] = rk
    kv_ref[1] = dot(normed, wv_ref[...]).astype(BF16)


def q_body(x_ref, wq_ref, q_ref, rq_ref):
    normed = layer_stats(x_ref[...].astype(F32))[0].astype(BF16)
    q, rq = head_norm(dot(normed, wq_ref[...]), head_sum_matrix(), head_spread_matrix())
    q_ref[...] = q
    rq_ref[...] = rq


def space_body(x_ref, q_ref, kv_ref, kvo_ref, wo_ref, out_ref, mixed_ref):
    def step(h, carry):
        win, keep = head_window(h)
        qm = jnp.where(keep, q_ref[:, win], 0.0).astype(BF16)
        total, out = 0.0, 0.0
        for ref in (kv_ref, kvo_ref):
            s = dot(qm, ref[0, :, win], NT)
            e = jnp.exp(s * SCALE)
            total = total + jnp.sum(e, axis=-1, keepdims=True)
            out = out + dot(e.astype(BF16), ref[1, :, win])
        out = out * (1.0 / total)
        mixed_ref[:, win] = jnp.where(keep, out, mixed_ref[:, win])
        return carry

    for h in range(HEADS):
        step(h, 0)
    out = x_ref[...].astype(F32) + dot(mixed_ref[...].astype(BF16), wo_ref[...])
    out_ref[...] = out.astype(BF16)


def back_body(g_ref, q_ref, kv_ref, kvo_ref, wo_ref, dq_ref, dkv_ref, dkvo_ref, do_ref, aq_ref, akv_ref):
    n = g_ref.shape[0]
    do_ref[...] = dot(g_ref[...], wo_ref[...], NT).astype(BF16)
    akv_ref[...] = jnp.zeros_like(akv_ref)

    def step(h, carry):
        win, keep = head_window(h)
        qm = jnp.where(keep, q_ref[:, win], 0.0).astype(BF16)
        dom = jnp.where(keep, do_ref[:, win], 0.0).astype(BF16)
        es, total = [], 0.0
        for ref in (kv_ref, kvo_ref):
            e = jnp.exp(dot(ref[0, :, win], qm, NT) * SCALE)
            total = total + jnp.sum(e, axis=0, keepdims=True)
            es.append(e)
        inv = 1.0 / total
        ps, dps, delta = [], [], 0.0
        for i, ref in enumerate((kv_ref, kvo_ref)):
            p = es[i] * inv
            dp = dot(ref[1, :, win], dom, NT)
            delta = delta + jnp.sum(p * dp, axis=0, keepdims=True)
            akv_ref[1, i, :, win] += dot(p.astype(BF16), dom)
            ps.append(p)
            dps.append(dp)
        dq = 0.0
        for i, ref in enumerate((kv_ref, kvo_ref)):
            ds = (ps[i] * (dps[i] - delta) * SCALE).astype(BF16)
            akv_ref[0, i, :, win] += dot(ds, qm)
            dq = dq + dot(ds, ref[0, :, win], TN)
        aq_ref[:, win] = jnp.where(keep, dq, aq_ref[:, win])
        return carry

    for h in range(HEADS):
        step(h, 0)
    dq_ref[...] = aq_ref[...].astype(BF16)
    for i in range(2):
        dkv_ref[i] = akv_ref[i, 0].astype(BF16)
        dkvo_ref[i] = akv_ref[i, 1].astype(BF16)


def final_body(x_ref, g_ref, q_ref, kv_ref, rq_ref, rk_ref, dq_ref, dkv_ref, got_ref, wq_ref, wk_ref, wv_ref, out_ref):
    sum_m, spread_m = head_sum_matrix(), head_spread_matrix()
    dq = head_norm_back(dq_ref[...].astype(F32), q_ref[...], rq_ref[...], sum_m, spread_m)
    grad = dot(dq, wq_ref[...], NT)
    dk = dkv_ref[0].astype(F32) + got_ref[0].astype(F32)
    dk = head_norm_back(dk, kv_ref[0], rk_ref[...], sum_m, spread_m)
    grad = grad + dot(dk, wk_ref[...], NT)
    dv = (dkv_ref[1].astype(F32) + got_ref[1].astype(F32)).astype(BF16)
    grad = grad + dot(dv, wv_ref[...], NT)
    normed, rstd = layer_stats(x_ref[...].astype(F32))
    out_ref[...] = (g_ref[...].astype(F32) + layer_back(grad, normed, rstd)).astype(BF16)


def time_body(
    x_ref, cot_ref, perm_ref, permt_ref, wq_ref, wk_ref, wv_ref, wo_ref,
    out_ref, grad_ref,
    q_ref, k_ref, v_ref, do_ref, mixed_ref, aq_ref, ak_ref, av_ref, mask_ref, g_ref,
):
    n = q_ref.shape[0]
    sum_m, spread_m = head_sum_matrix(), head_spread_matrix()
    normed = layer_stats(x_ref[pl.ds(0, n), :].astype(F32))[0].astype(BF16)
    q, rq = head_norm(dot(normed, wq_ref[...]), sum_m, spread_m)
    q_ref[...] = q
    k, rk = head_norm(dot(normed, wk_ref[...]), sum_m, spread_m)
    k_ref[...] = k
    v_ref[...] = dot(normed, wv_ref[...]).astype(BF16)
    g_ref[...] = dot(permt_ref[...], cot_ref[...]).astype(BF16)
    do_ref[...] = dot(g_ref[...], wo_ref[...], NT).astype(BF16)
    ak_ref[...] = jnp.zeros_like(ak_ref)
    av_ref[...] = jnp.zeros_like(av_ref)
    apart = lax.broadcasted_iota(jnp.int32, (n, n), 0) - lax.broadcasted_iota(jnp.int32, (n, n), 1)
    mask_ref[...] = jnp.where(lax.rem(apart, 6) == 0, 1.0, 0.0)

    def step(h, carry):
        win, keep = head_window(h)
        qm = jnp.where(keep, q_ref[:, win], 0.0).astype(BF16)
        dom = jnp.where(keep, do_ref[:, win], 0.0).astype(BF16)
        k, v = k_ref[:, win], v_ref[:, win]
        e = jnp.exp(dot(k, qm, NT) * SCALE) * mask_ref[...]
        p = e * (1.0 / jnp.sum(e, axis=0, keepdims=True))
        dp = dot(v, dom, NT)
        delta = jnp.sum(p * dp, axis=0, keepdims=True)
        pb = p.astype(BF16)
        ds = (p * (dp - delta) * SCALE).astype(BF16)
        mixed_ref[:, win] = jnp.where(keep, dot(pb, v, TN), mixed_ref[:, win])
        av_ref[:, win] += dot(pb, dom)
        ak_ref[:, win] += dot(ds, qm)
        aq_ref[:, win] = jnp.where(keep, dot(ds, k, TN), aq_ref[:, win])
        return carry

    for h in range(HEADS):
        step(h, 0)
    x = x_ref[pl.ds(0, n), :].astype(F32)
    out = (x + dot(mixed_ref[...].astype(BF16), wo_ref[...])).astype(BF16)
    out_ref[...] = dot(perm_ref[...], out).astype(BF16)
    dq = head_norm_back(aq_ref[...], q_ref[...], rq, sum_m, spread_m)
    grad = dot(dq, wq_ref[...], NT)
    dk = head_norm_back(ak_ref[...], k_ref[...], rk, sum_m, spread_m)
    grad = grad + dot(dk, wk_ref[...], NT)
    grad = grad + dot(av_ref[...].astype(BF16), wv_ref[...], NT)
    normed, rstd = layer_stats(x)
    grad_ref[pl.ds(0, n), :] = (g_ref[...].astype(F32) + layer_back(grad, normed, rstd)).astype(BF16)
    grad_ref[pl.ds(n, grad_ref.shape[0] - n), :] = jnp.zeros((grad_ref.shape[0] - n, D), BF16)


def perm_body(m_ref, a_ref, out_ref):
    out_ref[...] = dot(m_ref[...], a_ref[...]).astype(BF16)


def frame_permutation():
    m = np.zeros((320, 288), np.float32)
    for f in range(8):
        for c in range(6):
            for j in range(6):
                m[f * 40 + c * 6 + j, c * 48 + f * 6 + j] = 1.0
    return m


def local(tokens, cotangent, sq, sk, sv, so, tq, tk, tv, to):
    n, t = 384, 288
    swap = [(0, 1), (1, 0)]
    proj = 2 * n * D * D
    wb = 2 * D * D
    perm_np = frame_permutation()
    perm = jnp.asarray(perm_np, BF16)
    permt = jnp.asarray(np.ascontiguousarray(perm_np.T), BF16)

    x = jnp.pad(tokens, ((0, 2), (0, 0), (0, 0)))
    x = lax.all_to_all(x, "chip", 0, 0, tiled=True).reshape(n, D)

    cot = call(perm_body, sds((320, D)), [], 2 * 320 * t * D, 4 * t * D, "cot_pack")(
        perm, cotangent.reshape(t, D)
    )
    cot = lax.all_to_all(cot.reshape(8, 40, D), "frame", 0, 0, tiled=True).reshape(320, D)

    kv, rk = call(kv_body, (sds((2, n, D)), sds((n, 128), F32)), [], 2 * proj, 2 * wb, "space_kv")(x, sk, sv)
    kvo = lax.ppermute(kv, "core", swap)
    q, rq = call(q_body, (sds((n, D)), sds((n, 128), F32)), [], proj, wb, "space_q")(x, sq)
    q, cot = lax.optimization_barrier((q, cot))
    spaced = call(space_body, sds((n, D)), [pltpu.VMEM((n, D), F32)], 12 * proj, 2 * wb, "space_mix")(
        x, q, kv, kvo, so
    )

    tx = lax.all_to_all(spaced.reshape(64, 2, 3 * D), ("chip", "frame"), 0, 0, tiled=True).reshape(n, D)
    tout, tgrad = call(
        time_body,
        (sds((320, D)), sds((n, D))),
        [pltpu.VMEM((t, D), BF16)] * 4 + [pltpu.VMEM((t, D), F32)] * 4 + [pltpu.VMEM((t, t), F32), pltpu.VMEM((t, D), BF16)],
        20 * proj,
        4 * wb,
        "time",
    )(tx, cot, perm, permt, tq, tk, tv, to)
    g = lax.all_to_all(tgrad.reshape(64, 2, 3 * D), ("chip", "frame"), 0, 0, tiled=True).reshape(n, D)
    tout = lax.all_to_all(tout.reshape(8, 40, D), "frame", 0, 0, tiled=True).reshape(320, D)
    block = call(perm_body, sds((t, D)), [], 2 * 320 * t * D, 4 * t * D, "out_unpack")(permt, tout)

    dq, dkv, dkvo = call(
        back_body,
        (sds((n, D)), sds((2, n, D)), sds((2, n, D))),
        [pltpu.VMEM((n, D), BF16), pltpu.VMEM((n, D), F32), pltpu.VMEM((2, 2, n, D), F32)],
        20 * proj,
        2 * wb,
        "space_back",
    )(g, q, kv, kvo, so)
    got = lax.ppermute(dkvo, "core", swap)
    grad = call(final_body, sds((n, D)), [], 3 * proj, 4 * wb, "space_final")(
        x, g, q, kv, rq, rk, dq, dkv, got, sq, sk, sv
    )
    grad = lax.all_to_all(grad.reshape(8, 48, D), "chip", 0, 0, tiled=True)[:6]
    return block.reshape(6, 48, D), grad


def solution(mesh):
    planes = Mesh(mesh.devices.reshape(8, 8, 2), ("frame", "chip", "core"))
    spec = P("frame", ("chip", "core"), None)
    return jax.shard_map(
        local,
        mesh=planes,
        in_specs=(spec, spec) + (P(),) * 8,
        out_specs=(spec, spec),
        check_vma=False,
    )
```

```python
import functools
import math

import jax
import jax.numpy as jnp
import numpy as np
from jax import lax
from jax.experimental import pallas as pl
from jax.experimental.pallas import tpu as pltpu
from jax.sharding import Mesh
from jax.sharding import PartitionSpec as P

D = 1152
HEADS = 16
HD = D // HEADS
WIN = 256
EPS = 1e-6
SCALE = 1.0 / math.sqrt(HD)
F32 = jnp.float32
BF16 = jnp.bfloat16
TIME_LIMIT, BACK_LIMIT = 56, 34

NN = (((1,), (0,)), ((), ()))
NT = (((1,), (1,)), ((), ()))
TN = (((0,), (0,)), ((), ()))


def dot(a, b, dims=NN):
    return lax.dot_general(a, b, dims, preferred_element_type=F32)


def head_sum_matrix():
    i = lax.broadcasted_iota(jnp.int32, (D, 128), 0)
    j = lax.broadcasted_iota(jnp.int32, (D, 128), 1) * HD
    return jnp.where((i >= j) & (i < j + HD), 1.0, 0.0).astype(BF16)


def head_spread_matrix():
    j = (lax.broadcasted_iota(jnp.int32, (256, D), 0) & 127) * HD
    i = lax.broadcasted_iota(jnp.int32, (256, D), 1)
    return jnp.where((i >= j) & (i < j + HD), 1.0, 0.0).astype(BF16)


def spread(r, spread_m):
    high = r.astype(BF16)
    low = (r - high.astype(F32)).astype(BF16)
    return dot(jnp.concatenate([high, low], axis=1), spread_m)


def layer_stats(x):
    mean = jnp.mean(x, axis=-1, keepdims=True)
    center = x - mean
    rstd = lax.rsqrt(jnp.mean(center * center, axis=-1, keepdims=True) + EPS)
    return center * rstd, rstd


def head_norm(z, sum_m, spread_m):
    s = dot((z * z).astype(BF16), sum_m)
    r = lax.rsqrt(s * (1.0 / HD) + EPS)
    return (z * spread(r, spread_m)).astype(BF16), r


def head_norm_back(dy, y, r, sum_m, spread_m):
    yf = y.astype(F32)
    m = dot((dy * yf).astype(BF16), sum_m) * (1.0 / HD)
    return (dy * spread(r, spread_m) - yf * spread(r * m, spread_m)).astype(BF16)


def layer_back(dy, normed, rstd):
    a = jnp.mean(dy, axis=-1, keepdims=True)
    b = jnp.mean(dy * normed, axis=-1, keepdims=True)
    return rstd * (dy - a - normed * b)


def head_window(h):
    start = min((h * HD) // 128 * 128, D - WIN)
    lane = lax.broadcasted_iota(jnp.int32, (1, WIN), 1) + start
    keep = (lane >= h * HD) & (lane < h * HD + HD)
    return pl.ds(start, WIN), keep


MIB = 1024 * 1024


def call(body, out_shape, scratch, flops, name, limit, in_hbm=0):
    def run(*args):
        n = len(args) - in_hbm
        placed = [pltpu.with_memory_space_constraint(a, pltpu.VMEM if i < n else pltpu.HBM) for i, a in enumerate(args)]
        return pl.pallas_call(
            body,
            out_shape=out_shape,
            in_specs=[pl.BlockSpec(memory_space=pltpu.VMEM)] * n + [pl.BlockSpec(memory_space=pltpu.HBM)] * in_hbm,
            scratch_shapes=list(scratch) + ([pltpu.SemaphoreType.DMA((24,))] if in_hbm else []),
            compiler_params=pltpu.CompilerParams(vmem_limit_bytes=limit * MIB),
            cost_estimate=pl.CostEstimate(flops=flops, bytes_accessed=8 * D * D, transcendentals=0),
            name=name,
        )(*placed)

    return run


def sds(shape, dtype=BF16):
    return jax.ShapeDtypeStruct(shape, dtype)


def vmem(*shape, dtype=BF16):
    return pltpu.VMEM(shape, dtype)


class Fetch:
    def __init__(self, sems):
        self.sems, self.count, self.waiting = sems, 0, {}

    def start(self, key, src, dst):
        copy = pltpu.make_async_copy(src, dst, self.sems.at[self.count])
        self.count += 1
        copy.start()
        self.waiting.setdefault(key, []).append(copy)

    def wait(self, *keys):
        for key in keys:
            for copy in self.waiting.pop(key, ()):
                copy.wait()


COLS = D // 3


def last_column_group(h):
    start = min((h * HD) // 128 * 128, D - WIN)
    return (start + WIN - 1) // COLS


def entry_body(m_ref, a_ref, s0, s1, s2, s3, out_ref, t0, t1, t2, t3, sems):
    get = Fetch(sems)
    for src, dst in ((s0, t0), (s1, t1), (s2, t2), (s3, t3)):
        get.start("w", src, dst)
    out_ref[...] = dot(m_ref[...], a_ref[...]).astype(BF16)
    get.wait("w")


def perm_body(m_ref, a_ref, out_ref):
    out_ref[...] = dot(m_ref[...], a_ref[...]).astype(BF16)


def kv_body(x_ref, wk_ref, wv_ref, kv_ref, rk_ref):
    normed = layer_stats(x_ref[...].astype(F32))[0].astype(BF16)
    sum_m, spread_m = head_sum_matrix(), head_spread_matrix()
    k, rk = head_norm(dot(normed, wk_ref[...]), sum_m, spread_m)
    kv_ref[0] = k
    rk_ref[...] = rk
    kv_ref[1] = dot(normed, wv_ref[...]).astype(BF16)


def q_body(x_ref, wq_ref, q_ref, rq_ref):
    normed = layer_stats(x_ref[...].astype(F32))[0].astype(BF16)
    q, rq = head_norm(dot(normed, wq_ref[...]), head_sum_matrix(), head_spread_matrix())
    q_ref[...] = q
    rq_ref[...] = rq


def space_body(x_ref, q_ref, kv_ref, kvo_ref, wo_ref, out_ref, mixed_ref):
    def step(h, carry):
        win, keep = head_window(h)
        qm = jnp.where(keep, q_ref[:, win], 0.0).astype(BF16)
        total, out = 0.0, 0.0
        for ref in (kv_ref, kvo_ref):
            s = dot(qm, ref[0, :, win], NT)
            e = jnp.exp(s * SCALE)
            total = total + jnp.sum(e, axis=-1, keepdims=True)
            out = out + dot(e.astype(BF16), ref[1, :, win])
        out = out * (1.0 / total)
        mixed_ref[:, win] = jnp.where(keep, out, mixed_ref[:, win])
        return carry

    for h in range(HEADS):
        step(h, 0)
    out = x_ref[...].astype(F32) + dot(mixed_ref[...].astype(BF16), wo_ref[...])
    out_ref[...] = out.astype(BF16)


def fetch_columns(get, q_hbm, kv_hbm, kvo_hbm, q_ref, kv_ref, kvo_ref):
    for c in range(3):
        cols = pl.ds(c * COLS, COLS)
        get.start(c, q_hbm.at[:, cols], q_ref.at[:, cols])
        get.start(c, kv_hbm.at[:, :, cols], kv_ref.at[:, :, cols])
        get.start(c, kvo_hbm.at[:, :, cols], kvo_ref.at[:, :, cols])


def back_body(
    g_hbm, q_hbm, kv_hbm, kvo_hbm, wo_hbm, x_hbm, rq_hbm, rk_hbm, wq_hbm, wk_hbm, wv_hbm,
    dq_ref, dkv_ref, dkvo_ref, g_ref, q_ref, kv_ref, x_ref, rq_ref, rk_ref, wq_ref, wk_ref, wv_ref,
    kvo_ref, wo_ref, do_ref, aq_ref, akv_ref, sems,
):
    get = Fetch(sems)
    get.start("g", g_hbm, g_ref)
    for c in range(3):
        rows = pl.ds(c * COLS, COLS)
        get.start(("o", c), wo_hbm.at[rows], wo_ref.at[rows])
    fetch_columns(get, q_hbm, kv_hbm, kvo_hbm, q_ref, kv_ref, kvo_ref)
    get.start("f", x_hbm, x_ref)
    get.start("f", rq_hbm, rq_ref)
    get.start("f", rk_hbm, rk_ref)
    get.start("f", wq_hbm, wq_ref)
    get.start("f", wk_hbm, wk_ref)
    get.start("f", wv_hbm, wv_ref)
    akv_ref[...] = jnp.zeros_like(akv_ref)
    get.wait("g")
    for c in range(3):
        get.wait(("o", c))
        rows = pl.ds(c * COLS, COLS)
        do_ref[:, rows] = dot(g_ref[...], wo_ref[rows, :], NT).astype(BF16)
    for h in range(HEADS):
        get.wait(*range(last_column_group(h) + 1))
        win, keep = head_window(h)
        qm = jnp.where(keep, q_ref[:, win], 0.0).astype(BF16)
        dom = jnp.where(keep, do_ref[:, win], 0.0).astype(BF16)
        es, total = [], 0.0
        for ref in (kv_ref, kvo_ref):
            e = jnp.exp(dot(ref[0, :, win], qm, NT) * SCALE)
            total = total + jnp.sum(e, axis=0, keepdims=True)
            es.append(e)
        inv = 1.0 / total
        ps, dps, delta = [], [], 0.0
        for i, ref in enumerate((kv_ref, kvo_ref)):
            p = es[i] * inv
            dp = dot(ref[1, :, win], dom, NT)
            delta = delta + jnp.sum(p * dp, axis=0, keepdims=True)
            akv_ref[1, i, :, win] += dot(p.astype(BF16), dom)
            ps.append(p)
            dps.append(dp)
        dq = 0.0
        for i, ref in enumerate((kv_ref, kvo_ref)):
            ds = (ps[i] * (dps[i] - delta) * SCALE).astype(BF16)
            akv_ref[0, i, :, win] += dot(ds, qm)
            dq = dq + dot(ds, ref[0, :, win], TN)
        aq_ref[:, win] = jnp.where(keep, dq, aq_ref[:, win])
    dq_ref[...] = aq_ref[...].astype(BF16)
    for i in range(2):
        dkv_ref[i] = akv_ref[i, 0].astype(BF16)
        dkvo_ref[i] = akv_ref[i, 1].astype(BF16)
    get.wait("f")


def final_body(x_ref, g_ref, q_ref, kv_ref, rq_ref, rk_ref, dq_ref, dkv_ref, got_ref, wq_ref, wk_ref, wv_ref, out_ref):
    sum_m, spread_m = head_sum_matrix(), head_spread_matrix()
    dq = head_norm_back(dq_ref[...].astype(F32), q_ref[...], rq_ref[...], sum_m, spread_m)
    grad = dot(dq, wq_ref[...], NT)
    dk = dkv_ref[0].astype(F32) + got_ref[0].astype(F32)
    dk = head_norm_back(dk, kv_ref[0], rk_ref[...], sum_m, spread_m)
    grad = grad + dot(dk, wk_ref[...], NT)
    dv = (dkv_ref[1].astype(F32) + got_ref[1].astype(F32)).astype(BF16)
    grad = grad + dot(dv, wv_ref[...], NT)
    normed, rstd = layer_stats(x_ref[...].astype(F32))
    out_ref[...] = (g_ref[...].astype(F32) + layer_back(grad, normed, rstd)).astype(BF16)


def time_body(
    x_hbm, cot_hbm, perm_hbm, permt_hbm, wq_hbm, wk_hbm, wv_hbm, wo_hbm,
    out_ref, grad_ref,
    x_ref, cot_ref, perm_ref, permt_ref, wq_ref, wk_ref, wv_ref, wo_ref,
    q_ref, k_ref, v_ref, do_ref, mixed_ref, aq_ref, ak_ref, av_ref, mask_ref, g_ref, sems,
):
    n = q_ref.shape[0]
    get = Fetch(sems)
    get.start("x", x_hbm.at[pl.ds(0, n)], x_ref)
    get.start("q", wq_hbm, wq_ref)
    get.start("k", wk_hbm, wk_ref)
    get.start("v", wv_hbm, wv_ref)
    get.start("c", cot_hbm, cot_ref)
    get.start("c", permt_hbm, permt_ref)
    get.start("o", wo_hbm, wo_ref)
    get.start("p", perm_hbm, perm_ref)
    sum_m, spread_m = head_sum_matrix(), head_spread_matrix()
    ak_ref[...] = jnp.zeros_like(ak_ref)
    av_ref[...] = jnp.zeros_like(av_ref)
    apart = lax.broadcasted_iota(jnp.int32, (n, n), 0) - lax.broadcasted_iota(jnp.int32, (n, n), 1)
    mask_ref[...] = jnp.where(lax.rem(apart, 6) == 0, 1.0, 0.0)
    get.wait("x")
    normed = layer_stats(x_ref[...].astype(F32))[0].astype(BF16)
    get.wait("q")
    q, rq = head_norm(dot(normed, wq_ref[...]), sum_m, spread_m)
    q_ref[...] = q
    get.wait("k")
    k, rk = head_norm(dot(normed, wk_ref[...]), sum_m, spread_m)
    k_ref[...] = k
    get.wait("v")
    v_ref[...] = dot(normed, wv_ref[...]).astype(BF16)
    get.wait("c")
    g_ref[...] = dot(permt_ref[...], cot_ref[...]).astype(BF16)
    get.wait("o")
    do_ref[...] = dot(g_ref[...], wo_ref[...], NT).astype(BF16)

    for h in range(HEADS):
        win, keep = head_window(h)
        qm = jnp.where(keep, q_ref[:, win], 0.0).astype(BF16)
        dom = jnp.where(keep, do_ref[:, win], 0.0).astype(BF16)
        k, v = k_ref[:, win], v_ref[:, win]
        e = jnp.exp(dot(k, qm, NT) * SCALE) * mask_ref[...]
        p = e * (1.0 / jnp.sum(e, axis=0, keepdims=True))
        dp = dot(v, dom, NT)
        delta = jnp.sum(p * dp, axis=0, keepdims=True)
        pb = p.astype(BF16)
        ds = (p * (dp - delta) * SCALE).astype(BF16)
        mixed_ref[:, win] = jnp.where(keep, dot(pb, v, TN), mixed_ref[:, win])
        av_ref[:, win] += dot(pb, dom)
        ak_ref[:, win] += dot(ds, qm)
        aq_ref[:, win] = jnp.where(keep, dot(ds, k, TN), aq_ref[:, win])

    x = x_ref[...].astype(F32)
    out = (x + dot(mixed_ref[...].astype(BF16), wo_ref[...])).astype(BF16)
    get.wait("p")
    out_ref[...] = dot(perm_ref[...], out).astype(BF16)
    dq = head_norm_back(aq_ref[...], q_ref[...], rq, sum_m, spread_m)
    grad = dot(dq, wq_ref[...], NT)
    dk = head_norm_back(ak_ref[...], k_ref[...], rk, sum_m, spread_m)
    grad = grad + dot(dk, wk_ref[...], NT)
    grad = grad + dot(av_ref[...].astype(BF16), wv_ref[...], NT)
    normed, rstd = layer_stats(x)
    grad_ref[pl.ds(0, n), :] = (g_ref[...].astype(F32) + layer_back(grad, normed, rstd)).astype(BF16)
    grad_ref[pl.ds(n, grad_ref.shape[0] - n), :] = jnp.zeros((grad_ref.shape[0] - n, D), BF16)


def frame_permutation():
    m = np.zeros((320, 288), np.float32)
    for f in range(8):
        for c in range(6):
            for j in range(6):
                m[f * 40 + c * 6 + j, c * 48 + f * 6 + j] = 1.0
    return m


def local(tokens, cotangent, sq, sk, sv, so, tq, tk, tv, to):
    n, t = 384, 288
    swap = [(0, 1), (1, 0)]
    proj = 2 * n * D * D
    row, pair, norms, w = vmem(n, D), vmem(2, n, D), vmem(n, 128, dtype=F32), vmem(D, D)
    trow, tacc = vmem(t, D), vmem(t, D, dtype=F32)
    perm_np = frame_permutation()
    perm = jnp.asarray(perm_np, BF16)
    permt = jnp.asarray(np.ascontiguousarray(perm_np.T), BF16)

    x = jnp.pad(tokens, ((0, 2), (0, 0), (0, 0)))
    x = lax.all_to_all(x, "chip", 0, 0, tiled=True)
    cot, wq, wk, wv, wo = call(entry_body, (sds((320, D)), w, w, w, w), [], proj, "entry", 6, 4)(
        perm, cotangent.reshape(t, D), sq, sk, sv, so
    )
    x, cot, wq, wk, wv, wo = lax.optimization_barrier((x, cot, wq, wk, wv, wo))
    x = x.reshape(n, D)
    cot = lax.all_to_all(cot.reshape(8, 40, D), "frame", 0, 0, tiled=True)

    kv, rk = call(kv_body, (pair, norms), [], 2 * proj, "space_kv", 16)(x, wk, wv)
    kvo = lax.ppermute(kv, "core", swap)
    q, rq = call(q_body, (row, norms), [], proj, "space_q", 16)(x, wq)
    spaced = call(space_body, sds((n, D)), [vmem(n, D, dtype=F32)], 4 * proj, "space_mix", 16)(x, q, kv, kvo, wo)
    spaced, cot = lax.optimization_barrier((spaced, cot))

    tx = lax.all_to_all(spaced.reshape(64, 2, 3 * D), ("chip", "frame"), 0, 0, tiled=True).reshape(n, D)
    tout, tgrad = call(
        time_body,
        (sds((320, D)), sds((n, D))),
        [trow, vmem(320, D), vmem(320, t), vmem(t, 320), w, w, w, w]
        + [trow] * 4 + [tacc] * 4 + [vmem(t, t, dtype=F32), trow],
        10 * proj,
        "time",
        TIME_LIMIT,
        8,
    )(tx, cot.reshape(320, D), perm, permt, tq, tk, tv, to)
    g = lax.all_to_all(tgrad.reshape(64, 2, 3 * D), ("chip", "frame"), 0, 0, tiled=True).reshape(n, D)
    tout = lax.all_to_all(tout.reshape(8, 40, D), "frame", 0, 0, tiled=True).reshape(320, D)
    block = call(perm_body, sds((t, D)), [], proj // 2, "out_unpack", 6)(permt, tout)

    dq, dkv, dkvo, gf, qf, kvf, xf, rqf, rkf, wq, wk, wv = call(
        back_body,
        (row, pair, pair, row, row, pair, row, norms, norms, w, w, w),
        [pair, w, row, vmem(n, D, dtype=F32), vmem(2, 2, n, D, dtype=F32)],
        10 * proj,
        "space_back",
        BACK_LIMIT,
        11,
    )(g, q, kv, kvo, so, x, rq, rk, sq, sk, sv)
    got = lax.ppermute(dkvo, "core", swap)
    grad = call(final_body, sds((n, D)), [], 3 * proj, "space_final", 16)(
        xf, gf, qf, kvf, rqf, rkf, dq, dkv, got, wq, wk, wv
    )
    grad = lax.all_to_all(grad.reshape(8, 48, D), "chip", 0, 0, tiled=True)[:6]
    return block.reshape(6, 48, D), grad


def solution(mesh):
    planes = Mesh(mesh.devices.reshape(8, 8, 2), ("frame", "chip", "core"))
    spec = P("frame", ("chip", "core"), None)
    return jax.shard_map(
        local,
        mesh=planes,
        in_specs=(spec, spec) + (P(),) * 8,
        out_specs=(spec, spec),
        check_vma=False,
    )
```

```python
import functools
import math

import jax
import jax.numpy as jnp
import numpy as np
from jax import lax
from jax.experimental import pallas as pl
from jax.experimental.pallas import tpu as pltpu
from jax.sharding import Mesh
from jax.sharding import PartitionSpec as P

D = 1152
HEADS = 16
HD = D // HEADS
WIN = 256
EPS = 1e-6
SCALE = 1.0 / math.sqrt(HD)
F32 = jnp.float32
BF16 = jnp.bfloat16
TIME_LIMIT, BACK_LIMIT = 56, 34

NN = (((1,), (0,)), ((), ()))
NT = (((1,), (1,)), ((), ()))
TN = (((0,), (0,)), ((), ()))


def dot(a, b, dims=NN):
    return lax.dot_general(a, b, dims, preferred_element_type=F32)


def head_sum_matrix():
    i = lax.broadcasted_iota(jnp.int32, (D, 128), 0)
    j = lax.broadcasted_iota(jnp.int32, (D, 128), 1) * HD
    return jnp.where((i >= j) & (i < j + HD), 1.0, 0.0).astype(BF16)


def head_spread_matrix():
    j = (lax.broadcasted_iota(jnp.int32, (256, D), 0) & 127) * HD
    i = lax.broadcasted_iota(jnp.int32, (256, D), 1)
    return jnp.where((i >= j) & (i < j + HD), 1.0, 0.0).astype(BF16)


def spread(r, spread_m):
    high = r.astype(BF16)
    low = (r - high.astype(F32)).astype(BF16)
    return dot(jnp.concatenate([high, low], axis=1), spread_m)


def layer_stats(x):
    mean = jnp.mean(x, axis=-1, keepdims=True)
    center = x - mean
    rstd = lax.rsqrt(jnp.mean(center * center, axis=-1, keepdims=True) + EPS)
    return center * rstd, rstd


def head_norm(z, sum_m, spread_m):
    s = dot((z * z).astype(BF16), sum_m)
    r = lax.rsqrt(s * (1.0 / HD) + EPS)
    return (z * spread(r, spread_m)).astype(BF16), r


def head_norm_back(dy, y, r, sum_m, spread_m):
    yf = y.astype(F32)
    m = dot((dy * yf).astype(BF16), sum_m) * (1.0 / HD)
    return (dy * spread(r, spread_m) - yf * spread(r * m, spread_m)).astype(BF16)


def layer_back(dy, normed, rstd):
    a = jnp.mean(dy, axis=-1, keepdims=True)
    b = jnp.mean(dy * normed, axis=-1, keepdims=True)
    return rstd * (dy - a - normed * b)


def head_window(h):
    start = min((h * HD) // 128 * 128, D - WIN)
    lane = lax.broadcasted_iota(jnp.int32, (1, WIN), 1) + start
    keep = (lane >= h * HD) & (lane < h * HD + HD)
    return pl.ds(start, WIN), keep


MIB = 1024 * 1024


def call(body, out_shape, scratch, flops, name, limit, in_hbm=0):
    def run(*args):
        n = len(args) - in_hbm
        placed = [pltpu.with_memory_space_constraint(a, pltpu.VMEM if i < n else pltpu.HBM) for i, a in enumerate(args)]
        return pl.pallas_call(
            body,
            out_shape=out_shape,
            out_specs=jax.tree.map(lambda _: pl.BlockSpec(memory_space=pltpu.VMEM), out_shape, is_leaf=lambda o: hasattr(o, "shape")),
            in_specs=[pl.BlockSpec(memory_space=pltpu.VMEM)] * n + [pl.BlockSpec(memory_space=pltpu.HBM)] * in_hbm,
            scratch_shapes=list(scratch) + ([pltpu.SemaphoreType.DMA((24,))] if in_hbm else []),
            compiler_params=pltpu.CompilerParams(vmem_limit_bytes=limit * MIB),
            cost_estimate=pl.CostEstimate(flops=flops, bytes_accessed=8 * D * D, transcendentals=0),
            name=name,
        )(*placed)

    return run


def sds(shape, dtype=BF16):
    return jax.ShapeDtypeStruct(shape, dtype)


def hbm(*shape, dtype=BF16):
    return pltpu.HBM(shape, dtype)


def vmem(*shape, dtype=BF16):
    return pltpu.VMEM(shape, dtype)


class Fetch:
    def __init__(self, sems):
        self.sems, self.count, self.waiting = sems, 0, {}

    def start(self, key, src, dst):
        copy = pltpu.make_async_copy(src, dst, self.sems.at[self.count])
        self.count += 1
        copy.start()
        self.waiting.setdefault(key, []).append(copy)

    def wait(self, *keys):
        for key in keys:
            for copy in self.waiting.pop(key, ()):
                copy.wait()


COLS = D // 3


def entry_body(x_ref, out_ref):
    out_ref[pl.ds(0, 6)] = x_ref[...]
    out_ref[pl.ds(6, 2)] = jnp.zeros((2,) + x_ref.shape[1:], BF16)


def perm_body(m_ref, a_ref, out_ref):
    out_ref[...] = dot(m_ref[...], a_ref[...]).astype(BF16)


def kv_body(x_hbm, wk_hbm, wv_hbm, kv_ref, rk_ref, x_ref, wk_ref, wv_ref, sems):
    get = Fetch(sems)
    get.start("x", x_hbm, x_ref)
    get.start("k", wk_hbm, wk_ref)
    sum_m, spread_m = head_sum_matrix(), head_spread_matrix()
    get.wait("x")
    get.start("v", wv_hbm, wv_ref)
    normed = layer_stats(x_ref[...].astype(F32))[0].astype(BF16)
    get.wait("k")
    k, rk = head_norm(dot(normed, wk_ref[...]), sum_m, spread_m)
    kv_ref[0] = k
    rk_ref[...] = rk
    get.wait("v")
    kv_ref[1] = dot(normed, wv_ref[...]).astype(BF16)


def q_body(x_hbm, wq_hbm, wo_hbm, q_ref, rq_ref, x_ref, wo_ref, wq_ref, sems):
    get = Fetch(sems)
    get.start("x", x_hbm, x_ref)
    get.start("q", wq_hbm, wq_ref)
    sum_m, spread_m = head_sum_matrix(), head_spread_matrix()
    get.wait("x")
    get.start("o", wo_hbm, wo_ref)
    normed = layer_stats(x_ref[...].astype(F32))[0].astype(BF16)
    get.wait("q")
    q, rq = head_norm(dot(normed, wq_ref[...]), sum_m, spread_m)
    q_ref[...] = q
    rq_ref[...] = rq
    get.wait("o")


def space_body(q_ref, kv_ref, x_ref, wo_ref, kvo_hbm, out_ref, kvo_ref, mixed_ref, sems):
    get = Fetch(sems)
    get.start("k", kvo_hbm.at[0], kvo_ref.at[0])
    get.start("k", kvo_hbm.at[1], kvo_ref.at[1])
    get.wait("k")
    def step(h, carry):
        win, keep = head_window(h)
        qm = jnp.where(keep, q_ref[:, win], 0.0).astype(BF16)
        total, out = 0.0, 0.0
        for ref in (kv_ref, kvo_ref):
            s = dot(qm, ref[0, :, win], NT)
            e = jnp.exp(s * SCALE)
            total = total + jnp.sum(e, axis=-1, keepdims=True)
            out = out + dot(e.astype(BF16), ref[1, :, win])
        out = out * (1.0 / total)
        mixed_ref[:, win] = jnp.where(keep, out, mixed_ref[:, win])
        return carry

    for h in range(HEADS):
        step(h, 0)
    out = x_ref[...].astype(F32) + dot(mixed_ref[...].astype(BF16), wo_ref[...])
    out_ref[...] = out.astype(BF16)


def do_body(g_hbm, wo_hbm, do_ref, g_ref, wo_ref, sems):
    get = Fetch(sems)
    rows = [pl.ds(c * COLS, COLS) for c in range(3)]
    get.start("g", g_hbm, g_ref)
    for c in range(3):
        get.start(c, wo_hbm.at[rows[c]], wo_ref.at[rows[c]])
    get.wait("g")
    for c in range(3):
        get.wait(c)
        do_ref[:, rows[c]] = dot(g_ref[...], wo_ref[rows[c], :], NT).astype(BF16)


def back_body(
    g_hbm, q_hbm, kv_hbm, kvo_hbm, do_hbm, x_hbm, rq_hbm, rk_hbm, wq_hbm, wk_hbm, wv_hbm,
    dq_ref, dkv_ref, dkvo_ref, g_ref, q_ref, kv_ref, x_ref, rq_ref, rk_ref, wq_ref, wk_ref, wv_ref,
    kvo_ref, do_ref, aq_ref, akv_ref, sems,
):
    get = Fetch(sems)
    get.start("a", q_hbm, q_ref)
    get.start("a", kv_hbm, kv_ref)
    get.start("a", kvo_hbm, kvo_ref)
    get.start("a", do_hbm, do_ref)
    akv_ref[...] = jnp.zeros_like(akv_ref)
    get.wait("a")
    later = [(x_hbm, x_ref), (g_hbm, g_ref), (wq_hbm, wq_ref), (wk_hbm, wk_ref), (wv_hbm, wv_ref)]
    for src, dst in later + [(rq_hbm, rq_ref), (rk_hbm, rk_ref)]:
        get.start("f", src, dst)
    for h in range(HEADS):
        win, keep = head_window(h)
        qm = jnp.where(keep, q_ref[:, win], 0.0).astype(BF16)
        es, total = [], 0.0
        for ref in (kv_ref, kvo_ref):
            e = jnp.exp(dot(ref[0, :, win], qm, NT) * SCALE)
            total = total + jnp.sum(e, axis=0, keepdims=True)
            es.append(e)
        dom = jnp.where(keep, do_ref[:, win], 0.0).astype(BF16)
        inv = 1.0 / total
        ps, dps, delta = [], [], 0.0
        for i, ref in enumerate((kv_ref, kvo_ref)):
            p = es[i] * inv
            dp = dot(ref[1, :, win], dom, NT)
            delta = delta + jnp.sum(p * dp, axis=0, keepdims=True)
            akv_ref[1, i, :, win] += dot(p.astype(BF16), dom)
            ps.append(p)
            dps.append(dp)
        dq = 0.0
        for i, ref in enumerate((kv_ref, kvo_ref)):
            ds = (ps[i] * (dps[i] - delta) * SCALE).astype(BF16)
            akv_ref[0, i, :, win] += dot(ds, qm)
            dq = dq + dot(ds, ref[0, :, win], TN)
        aq_ref[:, win] = jnp.where(keep, dq, aq_ref[:, win])
    dq_ref[...] = aq_ref[...].astype(BF16)
    for i in range(2):
        dkv_ref[i] = akv_ref[i, 0].astype(BF16)
        dkvo_ref[i] = akv_ref[i, 1].astype(BF16)
    get.wait("f")


def final_q_body(q_ref, rq_ref, dq_ref, wq_ref, out_ref):
    sum_m, spread_m = head_sum_matrix(), head_spread_matrix()
    dq = head_norm_back(dq_ref[...].astype(F32), q_ref[...], rq_ref[...], sum_m, spread_m)
    out_ref[...] = dot(dq, wq_ref[...], NT)


def final_body(x_ref, g_ref, kv_ref, rk_ref, dkv_ref, part_ref, got_ref, wk_ref, wv_ref, out_ref):
    sum_m, spread_m = head_sum_matrix(), head_spread_matrix()
    dv = (dkv_ref[1].astype(F32) + got_ref[1].astype(F32)).astype(BF16)
    grad = part_ref[...] + dot(dv, wv_ref[...], NT)
    dk = dkv_ref[0].astype(F32) + got_ref[0].astype(F32)
    dk = head_norm_back(dk, kv_ref[0], rk_ref[...], sum_m, spread_m)
    grad = grad + dot(dk, wk_ref[...], NT)
    normed, rstd = layer_stats(x_ref[...].astype(F32))
    out_ref[...] = (g_ref[...].astype(F32) + layer_back(grad, normed, rstd)).astype(BF16)


def time_body(
    x_hbm, cot_hbm, perm_hbm, permt_hbm, wq_hbm, wk_hbm, wv_hbm, wo_hbm,
    out_ref, grad_ref,
    x_ref, cot_ref, perm_ref, permt_ref, wq_ref, wk_ref, wv_ref, wo_ref,
    q_ref, k_ref, v_ref, do_ref, mixed_ref, aq_ref, ak_ref, av_ref, mask_ref, g_ref, sems,
):
    n = q_ref.shape[0]
    get = Fetch(sems)
    get.start("x", x_hbm.at[pl.ds(0, n)], x_ref)
    get.start("q", wq_hbm, wq_ref)
    sum_m, spread_m = head_sum_matrix(), head_spread_matrix()
    ak_ref[...] = jnp.zeros_like(ak_ref)
    av_ref[...] = jnp.zeros_like(av_ref)
    apart = lax.broadcasted_iota(jnp.int32, (n, n), 0) - lax.broadcasted_iota(jnp.int32, (n, n), 1)
    mask_ref[...] = jnp.where(lax.rem(apart, 6) == 0, 1.0, 0.0)
    get.wait("x")
    get.start("k", wk_hbm, wk_ref)
    normed = layer_stats(x_ref[...].astype(F32))[0].astype(BF16)
    get.wait("q")
    get.start("v", wv_hbm, wv_ref)
    q, rq = head_norm(dot(normed, wq_ref[...]), sum_m, spread_m)
    q_ref[...] = q
    get.wait("k")
    get.start("c", cot_hbm, cot_ref)
    get.start("c", permt_hbm, permt_ref)
    k, rk = head_norm(dot(normed, wk_ref[...]), sum_m, spread_m)
    k_ref[...] = k
    get.wait("v")
    get.start("o", wo_hbm, wo_ref)
    v_ref[...] = dot(normed, wv_ref[...]).astype(BF16)
    get.wait("c")
    get.start("p", perm_hbm, perm_ref)
    g_ref[...] = dot(permt_ref[...], cot_ref[...]).astype(BF16)
    get.wait("o")
    do_ref[...] = dot(g_ref[...], wo_ref[...], NT).astype(BF16)

    for h in range(HEADS):
        win, keep = head_window(h)
        qm = jnp.where(keep, q_ref[:, win], 0.0).astype(BF16)
        dom = jnp.where(keep, do_ref[:, win], 0.0).astype(BF16)
        k, v = k_ref[:, win], v_ref[:, win]
        e = jnp.exp(dot(k, qm, NT) * SCALE) * mask_ref[...]
        p = e * (1.0 / jnp.sum(e, axis=0, keepdims=True))
        dp = dot(v, dom, NT)
        delta = jnp.sum(p * dp, axis=0, keepdims=True)
        pb = p.astype(BF16)
        ds = (p * (dp - delta) * SCALE).astype(BF16)
        mixed_ref[:, win] = jnp.where(keep, dot(pb, v, TN), mixed_ref[:, win])
        av_ref[:, win] += dot(pb, dom)
        ak_ref[:, win] += dot(ds, qm)
        aq_ref[:, win] = jnp.where(keep, dot(ds, k, TN), aq_ref[:, win])

    x = x_ref[...].astype(F32)
    out = (x + dot(mixed_ref[...].astype(BF16), wo_ref[...])).astype(BF16)
    get.wait("p")
    out_ref[...] = dot(perm_ref[...], out).astype(BF16)
    dq = head_norm_back(aq_ref[...], q_ref[...], rq, sum_m, spread_m)
    grad = dot(dq, wq_ref[...], NT)
    dk = head_norm_back(ak_ref[...], k_ref[...], rk, sum_m, spread_m)
    grad = grad + dot(dk, wk_ref[...], NT)
    grad = grad + dot(av_ref[...].astype(BF16), wv_ref[...], NT)
    normed, rstd = layer_stats(x)
    grad_ref[pl.ds(0, n), :] = (g_ref[...].astype(F32) + layer_back(grad, normed, rstd)).astype(BF16)
    grad_ref[pl.ds(n, grad_ref.shape[0] - n), :] = jnp.zeros((grad_ref.shape[0] - n, D), BF16)


def frame_permutation():
    m = np.zeros((320, 288), np.float32)
    for f in range(8):
        for c in range(6):
            for j in range(6):
                m[f * 40 + c * 6 + j, c * 48 + f * 6 + j] = 1.0
    return m


def local(tokens, cotangent, sq, sk, sv, so, tq, tk, tv, to):
    n, t = 384, 288
    swap = [(0, 1), (1, 0)]
    proj, small = 2 * n * D * D, 1 << 20
    row, pair, norms, w = vmem(n, D), vmem(2, n, D), vmem(n, 128, dtype=F32), vmem(D, D)
    trow, tacc = vmem(t, D), vmem(t, D, dtype=F32)
    perm_np = frame_permutation()
    perm = jnp.asarray(perm_np, BF16)
    permt = jnp.asarray(np.ascontiguousarray(perm_np.T), BF16)

    x = call(entry_body, sds((8, 48, D)), [], small, "entry", 6)(tokens)
    x = lax.all_to_all(x, "chip", 0, 0, tiled=True)
    cot = call(perm_body, sds((320, D)), [], proj // 2, "cot_pack", 6)(perm, cotangent.reshape(t, D))
    x, cot = lax.optimization_barrier((x, cot))
    x = x.reshape(n, D)
    cot = lax.all_to_all(cot.reshape(8, 40, D), "frame", 0, 0, tiled=True)

    kv, rk = call(kv_body, (pair, hbm(n, 128, dtype=F32)), [row, w, w], 2 * proj, "space_kv", 18, 3)(x, sk, sv)
    kvo = lax.ppermute(kv, "core", swap)
    q, rq, xv, wo = call(q_body, (row, hbm(n, 128, dtype=F32), row, w), [w], proj, "space_q", 14, 3)(x, sq, so)
    spaced = call(space_body, sds((n, D)), [pair, vmem(n, D, dtype=F32)], 4 * proj, "space_mix", 18, 1)(
        q, kv, xv, wo, kvo
    )
    spaced, cot = lax.optimization_barrier((spaced, cot))

    tx = lax.all_to_all(spaced.reshape(64, 2, 3 * D), ("chip", "frame"), 0, 0, tiled=True).reshape(n, D)
    tout, tgrad = call(
        time_body,
        (sds((320, D)), sds((n, D))),
        [trow, vmem(320, D), vmem(320, t), vmem(t, 320), w, w, w, w]
        + [trow] * 4 + [tacc] * 4 + [vmem(t, t, dtype=F32), trow],
        10 * proj,
        "time",
        TIME_LIMIT,
        8,
    )(tx, cot.reshape(320, D), perm, permt, tq, tk, tv, to)
    g = lax.all_to_all(tgrad.reshape(64, 2, 3 * D), ("chip", "frame"), 0, 0, tiled=True).reshape(n, D)
    tout = lax.all_to_all(tout.reshape(8, 40, D), "frame", 0, 0, tiled=True).reshape(320, D)
    do = call(do_body, hbm(n, D), [row, w], 2 * proj, "space_do", 14, 2)(g, so)
    do, tout = lax.optimization_barrier((do, tout))
    block = call(perm_body, sds((t, D)), [], proj // 2, "out_unpack", 6)(permt, tout)

    dq, dkv, dkvo, gf, qf, kvf, xf, rqf, rkf, wq, wk, wv = call(
        back_body,
        (row, pair, pair, row, row, pair, row, norms, norms, w, w, w),
        [pair, row, vmem(n, D, dtype=F32), vmem(2, 2, n, D, dtype=F32)],
        10 * proj,
        "space_back",
        BACK_LIMIT,
        11,
    )(g, q, kv, kvo, do, x, rq, rk, sq, sk, sv)
    got = lax.ppermute(dkvo, "core", swap)
    part = call(final_q_body, vmem(n, D, dtype=F32), [], proj, "space_final_q", 12)(qf, rqf, dq, wq)
    grad = call(final_body, sds((n, D)), [], 2 * proj, "space_final", 16)(xf, gf, kvf, rkf, dkv, part, got, wk, wv)
    grad = lax.all_to_all(grad.reshape(8, 48, D), "chip", 0, 0, tiled=True)[:6]
    return block.reshape(6, 48, D), grad


def solution(mesh):
    planes = Mesh(mesh.devices.reshape(8, 8, 2), ("frame", "chip", "core"))
    spec = P("frame", ("chip", "core"), None)
    return jax.shard_map(
        local,
        mesh=planes,
        in_specs=(spec, spec) + (P(),) * 8,
        out_specs=(spec, spec),
        check_vma=False,
    )
```

```python
import functools
import math

import jax
import jax.numpy as jnp
import numpy as np
from jax import lax
from jax.experimental import pallas as pl
from jax.experimental.pallas import tpu as pltpu
from jax.sharding import Mesh
from jax.sharding import PartitionSpec as P

D = 1152
HEADS = 16
HD = D // HEADS
WIN = 256
EPS = 1e-6
SCALE = 1.0 / math.sqrt(HD)
F32 = jnp.float32
BF16 = jnp.bfloat16
TIME_LIMIT, BACK_LIMIT = 32, 34

NN = (((1,), (0,)), ((), ()))
NT = (((1,), (1,)), ((), ()))
TN = (((0,), (0,)), ((), ()))


def dot(a, b, dims=NN):
    return lax.dot_general(a, b, dims, preferred_element_type=F32)


def head_sum_matrix():
    i = lax.broadcasted_iota(jnp.int32, (D, 128), 0)
    j = lax.broadcasted_iota(jnp.int32, (D, 128), 1) * HD
    return jnp.where((i >= j) & (i < j + HD), 1.0, 0.0).astype(BF16)


def head_spread_matrix():
    j = (lax.broadcasted_iota(jnp.int32, (256, D), 0) & 127) * HD
    i = lax.broadcasted_iota(jnp.int32, (256, D), 1)
    return jnp.where((i >= j) & (i < j + HD), 1.0, 0.0).astype(BF16)


def spread(r, spread_m):
    high = r.astype(BF16)
    low = (r - high.astype(F32)).astype(BF16)
    return dot(jnp.concatenate([high, low], axis=1), spread_m)


def layer_stats(x):
    mean = jnp.mean(x, axis=-1, keepdims=True)
    center = x - mean
    rstd = lax.rsqrt(jnp.mean(center * center, axis=-1, keepdims=True) + EPS)
    return center * rstd, rstd


def head_norm(z, sum_m, spread_m):
    s = dot((z * z).astype(BF16), sum_m)
    r = lax.rsqrt(s * (1.0 / HD) + EPS)
    return (z * spread(r, spread_m)).astype(BF16), r


def head_norm_back(dy, y, r, sum_m, spread_m):
    yf = y.astype(F32)
    m = dot((dy * yf).astype(BF16), sum_m) * (1.0 / HD)
    return (dy * spread(r, spread_m) - yf * spread(r * m, spread_m)).astype(BF16)


def layer_back(dy, normed, rstd):
    a = jnp.mean(dy, axis=-1, keepdims=True)
    b = jnp.mean(dy * normed, axis=-1, keepdims=True)
    return rstd * (dy - a - normed * b)


def head_window(h):
    start = min((h * HD) // 128 * 128, D - WIN)
    lane = lax.broadcasted_iota(jnp.int32, (1, WIN), 1) + start
    keep = (lane >= h * HD) & (lane < h * HD + HD)
    return pl.ds(start, WIN), keep


MIB = 1024 * 1024


def call(body, out_shape, scratch, flops, name, limit, in_hbm=0):
    def run(*args):
        n = len(args) - in_hbm
        placed = [pltpu.with_memory_space_constraint(a, pltpu.VMEM if i < n else pltpu.HBM) for i, a in enumerate(args)]
        return pl.pallas_call(
            body,
            out_shape=out_shape,
            out_specs=jax.tree.map(lambda _: pl.BlockSpec(memory_space=pltpu.VMEM), out_shape, is_leaf=lambda o: hasattr(o, "shape")),
            in_specs=[pl.BlockSpec(memory_space=pltpu.VMEM)] * n + [pl.BlockSpec(memory_space=pltpu.HBM)] * in_hbm,
            scratch_shapes=list(scratch) + ([pltpu.SemaphoreType.DMA((24,))] if in_hbm else []),
            compiler_params=pltpu.CompilerParams(vmem_limit_bytes=limit * MIB),
            cost_estimate=pl.CostEstimate(flops=flops, bytes_accessed=8 * D * D, transcendentals=0),
            name=name,
        )(*placed)

    return run


def sds(shape, dtype=BF16):
    return jax.ShapeDtypeStruct(shape, dtype)


def hbm(*shape, dtype=BF16):
    return pltpu.HBM(shape, dtype)


def vmem(*shape, dtype=BF16):
    return pltpu.VMEM(shape, dtype)


class Fetch:
    def __init__(self, sems):
        self.sems, self.count, self.waiting = sems, 0, {}

    def start(self, key, src, dst):
        copy = pltpu.make_async_copy(src, dst, self.sems.at[self.count])
        self.count += 1
        copy.start()
        self.waiting.setdefault(key, []).append(copy)

    def wait(self, *keys):
        for key in keys:
            for copy in self.waiting.pop(key, ()):
                copy.wait()


COLS = D // 3


def entry_body(x_hbm, out_ref, sems):
    get = Fetch(sems)
    get.start("x", x_hbm, out_ref.at[pl.ds(0, 6)])
    out_ref[pl.ds(6, 2)] = jnp.zeros((2,) + x_hbm.shape[1:], BF16)
    get.wait("x")


def perm_body(m_ref, a_ref, out_ref):
    out_ref[...] = dot(m_ref[...], a_ref[...]).astype(BF16)


def kv_body(x_ref, wk_hbm, wv_hbm, kv_ref, rk_ref, xo_ref, wk_ref, wv_ref, sems):
    get = Fetch(sems)
    get.start("k", wk_hbm, wk_ref)
    get.start("v", wv_hbm, wv_ref)
    sum_m, spread_m = head_sum_matrix(), head_spread_matrix()
    xo_ref[...] = x_ref[...]
    normed = layer_stats(x_ref[...].astype(F32))[0].astype(BF16)
    get.wait("k")
    k, rk = head_norm(dot(normed, wk_ref[...]), sum_m, spread_m)
    kv_ref[0] = k
    rk_ref[...] = rk
    get.wait("v")
    kv_ref[1] = dot(normed, wv_ref[...]).astype(BF16)


def q_body(x_hbm, wq_hbm, wo_hbm, q_ref, rq_ref, x_ref, wo_ref, wq_ref, sems):
    get = Fetch(sems)
    get.start("x", x_hbm, x_ref)
    get.start("q", wq_hbm, wq_ref)
    sum_m, spread_m = head_sum_matrix(), head_spread_matrix()
    get.wait("x")
    get.start("o", wo_hbm, wo_ref)
    normed = layer_stats(x_ref[...].astype(F32))[0].astype(BF16)
    get.wait("q")
    q, rq = head_norm(dot(normed, wq_ref[...]), sum_m, spread_m)
    q_ref[...] = q
    rq_ref[...] = rq
    get.wait("o")


def space_body(q_ref, kv_ref, x_ref, wo_ref, kvo_hbm, out_ref, kvo_ref, mixed_ref, sems):
    get = Fetch(sems)
    get.start("k", kvo_hbm.at[0], kvo_ref.at[0])
    get.start("k", kvo_hbm.at[1], kvo_ref.at[1])
    get.wait("k")
    def step(h, carry):
        win, keep = head_window(h)
        qm = jnp.where(keep, q_ref[:, win], 0.0).astype(BF16)
        total, out = 0.0, 0.0
        for ref in (kv_ref, kvo_ref):
            s = dot(qm, ref[0, :, win], NT)
            e = jnp.exp(s * SCALE)
            total = total + jnp.sum(e, axis=-1, keepdims=True)
            out = out + dot(e.astype(BF16), ref[1, :, win])
        out = out * (1.0 / total)
        mixed_ref[:, win] = jnp.where(keep, out, mixed_ref[:, win])
        return carry

    for h in range(HEADS):
        step(h, 0)
    out = x_ref[...].astype(F32) + dot(mixed_ref[...].astype(BF16), wo_ref[...])
    out_ref[...] = out.astype(BF16)


def do_body(g_hbm, wo_hbm, do_ref, g_ref, wo_ref, sems):
    get = Fetch(sems)
    rows = [pl.ds(c * COLS, COLS) for c in range(3)]
    get.start("g", g_hbm, g_ref)
    for c in range(3):
        get.start(c, wo_hbm.at[rows[c]], wo_ref.at[rows[c]])
    get.wait("g")
    for c in range(3):
        get.wait(c)
        do_ref[:, rows[c]] = dot(g_ref[...], wo_ref[rows[c], :], NT).astype(BF16)


def back_body(
    g_hbm, q_hbm, kv_hbm, kvo_hbm, do_hbm, x_hbm, rq_hbm, rk_hbm, wq_hbm, wk_hbm, wv_hbm,
    dq_ref, dkv_ref, dkvo_ref, g_ref, q_ref, kv_ref, x_ref, rq_ref, rk_ref, wq_ref, wk_ref, wv_ref,
    kvo_ref, do_ref, aq_ref, akv_ref, sems,
):
    get = Fetch(sems)
    get.start("a", q_hbm, q_ref)
    get.start("a", kv_hbm, kv_ref)
    get.start("a", kvo_hbm, kvo_ref)
    get.start("a", do_hbm, do_ref)
    akv_ref[...] = jnp.zeros_like(akv_ref)
    get.wait("a")
    later = [(x_hbm, x_ref), (g_hbm, g_ref), (wq_hbm, wq_ref), (wk_hbm, wk_ref), (wv_hbm, wv_ref)]
    for src, dst in later + [(rq_hbm, rq_ref), (rk_hbm, rk_ref)]:
        get.start("f", src, dst)
    for h in range(HEADS):
        win, keep = head_window(h)
        qm = jnp.where(keep, q_ref[:, win], 0.0).astype(BF16)
        es, total = [], 0.0
        for ref in (kv_ref, kvo_ref):
            e = jnp.exp(dot(ref[0, :, win], qm, NT) * SCALE)
            total = total + jnp.sum(e, axis=0, keepdims=True)
            es.append(e)
        dom = jnp.where(keep, do_ref[:, win], 0.0).astype(BF16)
        inv = 1.0 / total
        ps, dps, delta = [], [], 0.0
        for i, ref in enumerate((kv_ref, kvo_ref)):
            p = es[i] * inv
            dp = dot(ref[1, :, win], dom, NT)
            delta = delta + jnp.sum(p * dp, axis=0, keepdims=True)
            akv_ref[1, i, :, win] += dot(p.astype(BF16), dom)
            ps.append(p)
            dps.append(dp)
        dq = 0.0
        for i, ref in enumerate((kv_ref, kvo_ref)):
            ds = (ps[i] * (dps[i] - delta) * SCALE).astype(BF16)
            akv_ref[0, i, :, win] += dot(ds, qm)
            dq = dq + dot(ds, ref[0, :, win], TN)
        aq_ref[:, win] = jnp.where(keep, dq, aq_ref[:, win])
    dq_ref[...] = aq_ref[...].astype(BF16)
    for i in range(2):
        dkv_ref[i] = akv_ref[i, 0].astype(BF16)
        dkvo_ref[i] = akv_ref[i, 1].astype(BF16)
    get.wait("f")


def final_q_body(q_ref, rq_ref, dq_ref, wq_ref, out_ref):
    sum_m, spread_m = head_sum_matrix(), head_spread_matrix()
    dq = head_norm_back(dq_ref[...].astype(F32), q_ref[...], rq_ref[...], sum_m, spread_m)
    out_ref[...] = dot(dq, wq_ref[...], NT)


def final_body(x_ref, g_ref, kv_ref, rk_ref, dkv_ref, part_ref, got_ref, wk_ref, wv_ref, out_ref):
    sum_m, spread_m = head_sum_matrix(), head_spread_matrix()
    dv = (dkv_ref[1].astype(F32) + got_ref[1].astype(F32)).astype(BF16)
    grad = part_ref[...] + dot(dv, wv_ref[...], NT)
    dk = dkv_ref[0].astype(F32) + got_ref[0].astype(F32)
    dk = head_norm_back(dk, kv_ref[0], rk_ref[...], sum_m, spread_m)
    grad = grad + dot(dk, wk_ref[...], NT)
    normed, rstd = layer_stats(x_ref[...].astype(F32))
    out_ref[...] = (g_ref[...].astype(F32) + layer_back(grad, normed, rstd)).astype(BF16)


def time_body(
    x_ref, cot_hbm, perm_hbm, permt_hbm, wq_hbm, wk_hbm, wv_hbm, wo_hbm,
    out_ref, grad_ref,
    cot_ref, perm_ref, permt_ref, wq_ref, wk_ref, wv_ref, wo_ref,
    q_ref, k_ref, v_ref, do_ref, mixed_ref, aq_ref, ak_ref, av_ref, mask_ref, g_ref, sems,
):
    n = q_ref.shape[0]
    get = Fetch(sems)
    get.start("q", wq_hbm, wq_ref)
    get.start("k", wk_hbm, wk_ref)
    sum_m, spread_m = head_sum_matrix(), head_spread_matrix()
    ak_ref[...] = jnp.zeros_like(ak_ref)
    av_ref[...] = jnp.zeros_like(av_ref)
    apart = lax.broadcasted_iota(jnp.int32, (n, n), 0) - lax.broadcasted_iota(jnp.int32, (n, n), 1)
    mask_ref[...] = jnp.where(lax.rem(apart, 6) == 0, 1.0, 0.0)
    normed = layer_stats(x_ref[pl.ds(0, n), :].astype(F32))[0].astype(BF16)
    get.wait("q")
    get.start("v", wv_hbm, wv_ref)
    q, rq = head_norm(dot(normed, wq_ref[...]), sum_m, spread_m)
    q_ref[...] = q
    get.wait("k")
    get.start("c", cot_hbm, cot_ref)
    get.start("c", permt_hbm, permt_ref)
    k, rk = head_norm(dot(normed, wk_ref[...]), sum_m, spread_m)
    k_ref[...] = k
    get.wait("v")
    get.start("o", wo_hbm, wo_ref)
    v_ref[...] = dot(normed, wv_ref[...]).astype(BF16)
    get.wait("c")
    get.start("p", perm_hbm, perm_ref)
    g_ref[...] = dot(permt_ref[...], cot_ref[...]).astype(BF16)
    get.wait("o")
    do_ref[...] = dot(g_ref[...], wo_ref[...], NT).astype(BF16)

    for h in range(HEADS):
        win, keep = head_window(h)
        qm = jnp.where(keep, q_ref[:, win], 0.0).astype(BF16)
        dom = jnp.where(keep, do_ref[:, win], 0.0).astype(BF16)
        k, v = k_ref[:, win], v_ref[:, win]
        e = jnp.exp(dot(k, qm, NT) * SCALE) * mask_ref[...]
        p = e * (1.0 / jnp.sum(e, axis=0, keepdims=True))
        dp = dot(v, dom, NT)
        delta = jnp.sum(p * dp, axis=0, keepdims=True)
        pb = p.astype(BF16)
        ds = (p * (dp - delta) * SCALE).astype(BF16)
        mixed_ref[:, win] = jnp.where(keep, dot(pb, v, TN), mixed_ref[:, win])
        av_ref[:, win] += dot(pb, dom)
        ak_ref[:, win] += dot(ds, qm)
        aq_ref[:, win] = jnp.where(keep, dot(ds, k, TN), aq_ref[:, win])

    x = x_ref[pl.ds(0, n), :].astype(F32)
    out = (x + dot(mixed_ref[...].astype(BF16), wo_ref[...])).astype(BF16)
    get.wait("p")
    out_ref[...] = dot(perm_ref[...], out).astype(BF16)
    dq = head_norm_back(aq_ref[...], q_ref[...], rq, sum_m, spread_m)
    grad = dot(dq, wq_ref[...], NT)
    dk = head_norm_back(ak_ref[...], k_ref[...], rk, sum_m, spread_m)
    grad = grad + dot(dk, wk_ref[...], NT)
    grad = grad + dot(av_ref[...].astype(BF16), wv_ref[...], NT)
    normed, rstd = layer_stats(x)
    grad_ref[pl.ds(0, n), :] = (g_ref[...].astype(F32) + layer_back(grad, normed, rstd)).astype(BF16)
    grad_ref[pl.ds(n, grad_ref.shape[0] - n), :] = jnp.zeros((grad_ref.shape[0] - n, D), BF16)


def frame_permutation():
    m = np.zeros((320, 288), np.float32)
    for f in range(8):
        for c in range(6):
            for j in range(6):
                m[f * 40 + c * 6 + j, c * 48 + f * 6 + j] = 1.0
    return m


def local(tokens, cotangent, sq, sk, sv, so, tq, tk, tv, to):
    n, t = 384, 288
    swap = [(0, 1), (1, 0)]
    proj, small = 2 * n * D * D, 1 << 20
    row, pair, norms, w = vmem(n, D), vmem(2, n, D), vmem(n, 128, dtype=F32), vmem(D, D)
    trow, tacc = vmem(t, D), vmem(t, D, dtype=F32)
    perm_np = frame_permutation()
    perm = jnp.asarray(perm_np, BF16)
    permt = jnp.asarray(np.ascontiguousarray(perm_np.T), BF16)

    x = call(entry_body, sds((8, 48, D)), [], small, "entry", 6, 1)(tokens)
    x = lax.all_to_all(x, "chip", 0, 0, tiled=True)
    cot = call(perm_body, sds((320, D)), [], proj // 2, "cot_pack", 6)(perm, cotangent.reshape(t, D))
    x, cot = lax.optimization_barrier((x, cot))
    x = x.reshape(n, D)
    cot = lax.all_to_all(cot.reshape(8, 40, D), "frame", 0, 0, tiled=True)

    kv, rk, x = call(
        kv_body, (pair, hbm(n, 128, dtype=F32), hbm(n, D)), [w, w], 2 * proj, "space_kv", 18, 2
    )(x, sk, sv)
    kvo = lax.ppermute(kv, "core", swap)
    q, rq, xv, wo = call(q_body, (row, hbm(n, 128, dtype=F32), row, w), [w], proj, "space_q", 14, 3)(x, sq, so)
    spaced = call(space_body, sds((n, D)), [pair, vmem(n, D, dtype=F32)], 4 * proj, "space_mix", 18, 1)(
        q, kv, xv, wo, kvo
    )
    spaced, cot = lax.optimization_barrier((spaced, cot))

    tx = lax.all_to_all(spaced.reshape(64, 2, 3 * D), ("chip", "frame"), 0, 0, tiled=True).reshape(n, D)
    tout, tgrad = call(
        time_body,
        (sds((320, D)), sds((n, D))),
        [vmem(320, D), vmem(320, t), vmem(t, 320), w, w, w, w]
        + [trow] * 4 + [tacc] * 4 + [vmem(t, t, dtype=F32), trow],
        10 * proj,
        "time",
        TIME_LIMIT,
        7,
    )(tx, cot.reshape(320, D), perm, permt, tq, tk, tv, to)
    g = lax.all_to_all(tgrad.reshape(64, 2, 3 * D), ("chip", "frame"), 0, 0, tiled=True).reshape(n, D)
    tout = lax.all_to_all(tout.reshape(8, 40, D), "frame", 0, 0, tiled=True).reshape(320, D)
    do = call(do_body, hbm(n, D), [row, w], 2 * proj, "space_do", 14, 2)(g, so)
    do, tout = lax.optimization_barrier((do, tout))
    block = call(perm_body, sds((t, D)), [], proj // 2, "out_unpack", 6)(permt, tout)

    dq, dkv, dkvo, gf, qf, kvf, xf, rqf, rkf, wq, wk, wv = call(
        back_body,
        (row, pair, pair, row, row, pair, row, norms, norms, w, w, w),
        [pair, row, vmem(n, D, dtype=F32), vmem(2, 2, n, D, dtype=F32)],
        10 * proj,
        "space_back",
        BACK_LIMIT,
        11,
    )(g, q, kv, kvo, do, x, rq, rk, sq, sk, sv)
    got = lax.ppermute(dkvo, "core", swap)
    part = call(final_q_body, vmem(n, D, dtype=F32), [], proj, "space_final_q", 12)(qf, rqf, dq, wq)
    grad = call(final_body, sds((n, D)), [], 2 * proj, "space_final", 16)(xf, gf, kvf, rkf, dkv, part, got, wk, wv)
    grad = lax.all_to_all(grad.reshape(8, 48, D), "chip", 0, 0, tiled=True)[:6]
    return block.reshape(6, 48, D), grad


def solution(mesh):
    planes = Mesh(mesh.devices.reshape(8, 8, 2), ("frame", "chip", "core"))
    spec = P("frame", ("chip", "core"), None)
    return jax.shard_map(
        local,
        mesh=planes,
        in_specs=(spec, spec) + (P(),) * 8,
        out_specs=(spec, spec),
        check_vma=False,
    )
```

```python
import functools
import math

import jax
import jax.numpy as jnp
import numpy as np
from jax import lax
from jax.experimental import pallas as pl
from jax.experimental.pallas import tpu as pltpu
from jax.sharding import Mesh
from jax.sharding import PartitionSpec as P

D = 1152
HEADS = 16
HD = D // HEADS
WIN = 256
EPS = 1e-6
SCALE = 1.0 / math.sqrt(HD)
F32 = jnp.float32
BF16 = jnp.bfloat16
TIME_LIMIT, BACK_LIMIT = 32, 34

NN = (((1,), (0,)), ((), ()))
NT = (((1,), (1,)), ((), ()))
TN = (((0,), (0,)), ((), ()))


def dot(a, b, dims=NN):
    return lax.dot_general(a, b, dims, preferred_element_type=F32)


def head_sum_matrix():
    i = lax.broadcasted_iota(jnp.int32, (D, 128), 0)
    j = lax.broadcasted_iota(jnp.int32, (D, 128), 1) * HD
    return jnp.where((i >= j) & (i < j + HD), 1.0, 0.0).astype(BF16)


def head_spread_matrix():
    j = (lax.broadcasted_iota(jnp.int32, (256, D), 0) & 127) * HD
    i = lax.broadcasted_iota(jnp.int32, (256, D), 1)
    return jnp.where((i >= j) & (i < j + HD), 1.0, 0.0).astype(BF16)


def spread(r, spread_m):
    high = r.astype(BF16)
    low = (r - high.astype(F32)).astype(BF16)
    return dot(jnp.concatenate([high, low], axis=1), spread_m)


def layer_stats(x):
    mean = jnp.mean(x, axis=-1, keepdims=True)
    center = x - mean
    rstd = lax.rsqrt(jnp.mean(center * center, axis=-1, keepdims=True) + EPS)
    return center * rstd, rstd


def head_norm(z, sum_m, spread_m):
    s = dot((z * z).astype(BF16), sum_m)
    r = lax.rsqrt(s * (1.0 / HD) + EPS)
    return (z * spread(r, spread_m)).astype(BF16), r


def head_norm_back(dy, y, r, sum_m, spread_m):
    yf = y.astype(F32)
    m = dot((dy * yf).astype(BF16), sum_m) * (1.0 / HD)
    return (dy * spread(r, spread_m) - yf * spread(r * m, spread_m)).astype(BF16)


def layer_back(dy, normed, rstd):
    a = jnp.mean(dy, axis=-1, keepdims=True)
    b = jnp.mean(dy * normed, axis=-1, keepdims=True)
    return rstd * (dy - a - normed * b)


def head_window(h):
    start = min((h * HD) // 128 * 128, D - WIN)
    lane = lax.broadcasted_iota(jnp.int32, (1, WIN), 1) + start
    keep = (lane >= h * HD) & (lane < h * HD + HD)
    return pl.ds(start, WIN), keep


MIB = 1024 * 1024


def call(body, out_shape, scratch, flops, name, limit, in_hbm=0):
    def run(*args):
        n = len(args) - in_hbm
        placed = [pltpu.with_memory_space_constraint(a, pltpu.VMEM if i < n else pltpu.HBM) for i, a in enumerate(args)]
        return pl.pallas_call(
            body,
            out_shape=out_shape,
            out_specs=jax.tree.map(lambda _: pl.BlockSpec(memory_space=pltpu.VMEM), out_shape, is_leaf=lambda o: hasattr(o, "shape")),
            in_specs=[pl.BlockSpec(memory_space=pltpu.VMEM)] * n + [pl.BlockSpec(memory_space=pltpu.HBM)] * in_hbm,
            scratch_shapes=list(scratch) + ([pltpu.SemaphoreType.DMA((24,))] if in_hbm else []),
            compiler_params=pltpu.CompilerParams(vmem_limit_bytes=limit * MIB),
            cost_estimate=pl.CostEstimate(flops=flops, bytes_accessed=8 * D * D, transcendentals=0),
            name=name,
        )(*placed)

    return run


def sds(shape, dtype=BF16):
    return jax.ShapeDtypeStruct(shape, dtype)


def hbm(*shape, dtype=BF16):
    return pltpu.HBM(shape, dtype)


def vmem(*shape, dtype=BF16):
    return pltpu.VMEM(shape, dtype)


class Fetch:
    def __init__(self, sems):
        self.sems, self.count, self.waiting = sems, 0, {}

    def start(self, key, src, dst):
        copy = pltpu.make_async_copy(src, dst, self.sems.at[self.count])
        self.count += 1
        copy.start()
        self.waiting.setdefault(key, []).append(copy)

    def wait(self, *keys):
        for key in keys:
            for copy in self.waiting.pop(key, ()):
                copy.wait()


COLS = D // 3


def entry_body(x_hbm, out_ref, sems):
    get = Fetch(sems)
    get.start("x", x_hbm, out_ref.at[pl.ds(0, 6)])
    out_ref[pl.ds(6, 2)] = jnp.zeros((2,) + x_hbm.shape[1:], BF16)
    get.wait("x")


def perm_body(m_ref, a_ref, out_ref):
    out_ref[...] = dot(m_ref[...], a_ref[...]).astype(BF16)


def kv_body(x_ref, wk_hbm, wv_hbm, kv_ref, rk_ref, xo_ref, wk_ref, wv_ref, sems):
    get = Fetch(sems)
    get.start("k", wk_hbm, wk_ref)
    get.start("v", wv_hbm, wv_ref)
    sum_m, spread_m = head_sum_matrix(), head_spread_matrix()
    xo_ref[...] = x_ref[...]
    normed = layer_stats(x_ref[...].astype(F32))[0].astype(BF16)
    get.wait("k")
    k, rk = head_norm(dot(normed, wk_ref[...]), sum_m, spread_m)
    kv_ref[0] = k
    rk_ref[...] = rk
    get.wait("v")
    kv_ref[1] = dot(normed, wv_ref[...]).astype(BF16)


def q_body(x_hbm, wq_hbm, wo_hbm, q_ref, rq_ref, x_ref, wo_ref, wq_ref, sems):
    get = Fetch(sems)
    get.start("x", x_hbm, x_ref)
    get.start("q", wq_hbm, wq_ref)
    sum_m, spread_m = head_sum_matrix(), head_spread_matrix()
    get.wait("x")
    get.start("o", wo_hbm, wo_ref)
    normed = layer_stats(x_ref[...].astype(F32))[0].astype(BF16)
    get.wait("q")
    q, rq = head_norm(dot(normed, wq_ref[...]), sum_m, spread_m)
    q_ref[...] = q
    rq_ref[...] = rq
    get.wait("o")


def space_body(q_ref, kv_ref, x_ref, wo_ref, kvo_hbm, out_ref, kvo_ref, mixed_ref, sems):
    get = Fetch(sems)
    get.start("k", kvo_hbm.at[0], kvo_ref.at[0])
    get.start("v", kvo_hbm.at[1], kvo_ref.at[1])
    def step(h, carry):
        win, keep = head_window(h)
        qm = jnp.where(keep, q_ref[:, win], 0.0).astype(BF16)
        total, out = 0.0, 0.0
        for ref in (kv_ref, kvo_ref):
            if h == 0 and ref is kvo_ref:
                get.wait("k", "v")
            s = dot(qm, ref[0, :, win], NT)
            e = jnp.exp(s * SCALE)
            total = total + jnp.sum(e, axis=-1, keepdims=True)
            out = out + dot(e.astype(BF16), ref[1, :, win])
        out = out * (1.0 / total)
        mixed_ref[:, win] = jnp.where(keep, out, mixed_ref[:, win])
        return carry

    for h in range(HEADS):
        step(h, 0)
    out = x_ref[...].astype(F32) + dot(mixed_ref[...].astype(BF16), wo_ref[...])
    out_ref[...] = out.astype(BF16)


def do_body(g_hbm, wo_hbm, do_ref, g_ref, wo_ref, sems):
    get = Fetch(sems)
    rows = [pl.ds(c * COLS, COLS) for c in range(3)]
    get.start("g", g_hbm, g_ref)
    for c in range(3):
        get.start(c, wo_hbm.at[rows[c]], wo_ref.at[rows[c]])
    get.wait("g")
    for c in range(3):
        get.wait(c)
        do_ref[:, rows[c]] = dot(g_ref[...], wo_ref[rows[c], :], NT).astype(BF16)


def back_body(
    g_hbm, q_hbm, kv_hbm, kvo_hbm, do_hbm, x_hbm, rq_hbm, rk_hbm, wq_hbm, wk_hbm, wv_hbm,
    dq_ref, dkv_ref, dkvo_ref, g_ref, q_ref, kv_ref, x_ref, rq_ref, rk_ref, wq_ref, wk_ref, wv_ref,
    kvo_ref, do_ref, aq_ref, akv_ref, sems,
):
    get = Fetch(sems)
    get.start("q", q_hbm, q_ref)
    get.start("q", kv_hbm.at[0], kv_ref.at[0])
    get.start("q", kvo_hbm.at[0], kvo_ref.at[0])
    akv_ref[...] = jnp.zeros_like(akv_ref)
    get.wait("q")
    get.start("v", do_hbm, do_ref)
    get.start("v", kv_hbm.at[1], kv_ref.at[1])
    get.start("v", kvo_hbm.at[1], kvo_ref.at[1])
    later = [(x_hbm, x_ref), (g_hbm, g_ref), (wq_hbm, wq_ref), (wk_hbm, wk_ref), (wv_hbm, wv_ref)]
    later += [(rq_hbm, rq_ref), (rk_hbm, rk_ref)]
    for h in range(HEADS):
        win, keep = head_window(h)
        qm = jnp.where(keep, q_ref[:, win], 0.0).astype(BF16)
        es, total = [], 0.0
        for ref in (kv_ref, kvo_ref):
            e = jnp.exp(dot(ref[0, :, win], qm, NT) * SCALE)
            total = total + jnp.sum(e, axis=0, keepdims=True)
            es.append(e)
        if h == 0:
            get.wait("v")
            for src, dst in later:
                get.start("f", src, dst)
        dom = jnp.where(keep, do_ref[:, win], 0.0).astype(BF16)
        inv = 1.0 / total
        ps, dps, delta = [], [], 0.0
        for i, ref in enumerate((kv_ref, kvo_ref)):
            p = es[i] * inv
            dp = dot(ref[1, :, win], dom, NT)
            delta = delta + jnp.sum(p * dp, axis=0, keepdims=True)
            akv_ref[1, i, :, win] += dot(p.astype(BF16), dom)
            ps.append(p)
            dps.append(dp)
        dq = 0.0
        for i, ref in enumerate((kv_ref, kvo_ref)):
            ds = (ps[i] * (dps[i] - delta) * SCALE).astype(BF16)
            akv_ref[0, i, :, win] += dot(ds, qm)
            dq = dq + dot(ds, ref[0, :, win], TN)
        aq_ref[:, win] = jnp.where(keep, dq, aq_ref[:, win])
    dq_ref[...] = aq_ref[...].astype(BF16)
    for i in range(2):
        dkv_ref[i] = akv_ref[i, 0].astype(BF16)
        dkvo_ref[i] = akv_ref[i, 1].astype(BF16)
    get.wait("f")


def final_q_body(q_ref, rq_ref, dq_ref, wq_ref, out_ref):
    sum_m, spread_m = head_sum_matrix(), head_spread_matrix()
    dq = head_norm_back(dq_ref[...].astype(F32), q_ref[...], rq_ref[...], sum_m, spread_m)
    out_ref[...] = dot(dq, wq_ref[...], NT)


def final_body(x_ref, g_ref, kv_ref, rk_ref, dkv_ref, part_ref, got_ref, wk_ref, wv_ref, out_ref):
    sum_m, spread_m = head_sum_matrix(), head_spread_matrix()
    dv = (dkv_ref[1].astype(F32) + got_ref[1].astype(F32)).astype(BF16)
    grad = part_ref[...] + dot(dv, wv_ref[...], NT)
    dk = dkv_ref[0].astype(F32) + got_ref[0].astype(F32)
    dk = head_norm_back(dk, kv_ref[0], rk_ref[...], sum_m, spread_m)
    grad = grad + dot(dk, wk_ref[...], NT)
    normed, rstd = layer_stats(x_ref[...].astype(F32))
    out_ref[...] = (g_ref[...].astype(F32) + layer_back(grad, normed, rstd)).astype(BF16)


def time_body(
    x_ref, cot_hbm, perm_hbm, permt_hbm, wq_hbm, wk_hbm, wv_hbm, wo_hbm,
    out_ref, grad_ref,
    cot_ref, perm_ref, permt_ref, wq_ref, wk_ref, wv_ref, wo_ref,
    q_ref, k_ref, v_ref, do_ref, mixed_ref, aq_ref, ak_ref, av_ref, mask_ref, g_ref, sems,
):
    n = q_ref.shape[0]
    get = Fetch(sems)
    get.start("q", wq_hbm, wq_ref)
    get.start("k", wk_hbm, wk_ref)
    sum_m, spread_m = head_sum_matrix(), head_spread_matrix()
    ak_ref[...] = jnp.zeros_like(ak_ref)
    av_ref[...] = jnp.zeros_like(av_ref)
    apart = lax.broadcasted_iota(jnp.int32, (n, n), 0) - lax.broadcasted_iota(jnp.int32, (n, n), 1)
    mask_ref[...] = jnp.where(lax.rem(apart, 6) == 0, 1.0, 0.0)
    normed = layer_stats(x_ref[pl.ds(0, n), :].astype(F32))[0].astype(BF16)
    get.wait("q")
    get.start("v", wv_hbm, wv_ref)
    q, rq = head_norm(dot(normed, wq_ref[...]), sum_m, spread_m)
    q_ref[...] = q
    get.wait("k")
    get.start("c", cot_hbm, cot_ref)
    get.start("c", permt_hbm, permt_ref)
    k, rk = head_norm(dot(normed, wk_ref[...]), sum_m, spread_m)
    k_ref[...] = k
    get.wait("v")
    get.start("o", wo_hbm, wo_ref)
    v_ref[...] = dot(normed, wv_ref[...]).astype(BF16)
    get.wait("c")
    get.start("p", perm_hbm, perm_ref)
    g_ref[...] = dot(permt_ref[...], cot_ref[...]).astype(BF16)
    get.wait("o")
    do_ref[...] = dot(g_ref[...], wo_ref[...], NT).astype(BF16)

    for h in range(HEADS):
        win, keep = head_window(h)
        qm = jnp.where(keep, q_ref[:, win], 0.0).astype(BF16)
        dom = jnp.where(keep, do_ref[:, win], 0.0).astype(BF16)
        k, v = k_ref[:, win], v_ref[:, win]
        e = jnp.exp(dot(k, qm, NT) * SCALE) * mask_ref[...]
        p = e * (1.0 / jnp.sum(e, axis=0, keepdims=True))
        dp = dot(v, dom, NT)
        delta = jnp.sum(p * dp, axis=0, keepdims=True)
        pb = p.astype(BF16)
        ds = (p * (dp - delta) * SCALE).astype(BF16)
        mixed_ref[:, win] = jnp.where(keep, dot(pb, v, TN), mixed_ref[:, win])
        av_ref[:, win] += dot(pb, dom)
        ak_ref[:, win] += dot(ds, qm)
        aq_ref[:, win] = jnp.where(keep, dot(ds, k, TN), aq_ref[:, win])

    x = x_ref[pl.ds(0, n), :].astype(F32)
    out = (x + dot(mixed_ref[...].astype(BF16), wo_ref[...])).astype(BF16)
    get.wait("p")
    out_ref[...] = dot(perm_ref[...], out).astype(BF16)
    dq = head_norm_back(aq_ref[...], q_ref[...], rq, sum_m, spread_m)
    grad = dot(dq, wq_ref[...], NT)
    dk = head_norm_back(ak_ref[...], k_ref[...], rk, sum_m, spread_m)
    grad = grad + dot(dk, wk_ref[...], NT)
    grad = grad + dot(av_ref[...].astype(BF16), wv_ref[...], NT)
    normed, rstd = layer_stats(x)
    grad_ref[pl.ds(0, n), :] = (g_ref[...].astype(F32) + layer_back(grad, normed, rstd)).astype(BF16)
    grad_ref[pl.ds(n, grad_ref.shape[0] - n), :] = jnp.zeros((grad_ref.shape[0] - n, D), BF16)


def frame_permutation():
    m = np.zeros((320, 288), np.float32)
    for f in range(8):
        for c in range(6):
            for j in range(6):
                m[f * 40 + c * 6 + j, c * 48 + f * 6 + j] = 1.0
    return m


def local(tokens, cotangent, sq, sk, sv, so, tq, tk, tv, to):
    n, t = 384, 288
    swap = [(0, 1), (1, 0)]
    proj, small = 2 * n * D * D, 1 << 20
    row, pair, norms, w = vmem(n, D), vmem(2, n, D), vmem(n, 128, dtype=F32), vmem(D, D)
    trow, tacc = vmem(t, D), vmem(t, D, dtype=F32)
    perm_np = frame_permutation()
    perm = jnp.asarray(perm_np, BF16)
    permt = jnp.asarray(np.ascontiguousarray(perm_np.T), BF16)

    x = call(entry_body, sds((8, 48, D)), [], small, "entry", 6, 1)(tokens)
    x = lax.all_to_all(x, "chip", 0, 0, tiled=True)
    cot = call(perm_body, sds((320, D)), [], proj // 2, "cot_pack", 6)(perm, cotangent.reshape(t, D))
    x, cot = lax.optimization_barrier((x, cot))
    x = x.reshape(n, D)
    cot = lax.all_to_all(cot.reshape(8, 40, D), "frame", 0, 0, tiled=True)

    kv, rk, x = call(
        kv_body, (pair, hbm(n, 128, dtype=F32), hbm(n, D)), [w, w], 2 * proj, "space_kv", 18, 2
    )(x, sk, sv)
    kvo = lax.ppermute(kv, "core", swap)
    q, rq, xv, wo = call(q_body, (row, hbm(n, 128, dtype=F32), row, w), [w], proj, "space_q", 14, 3)(x, sq, so)
    spaced = call(space_body, sds((n, D)), [pair, vmem(n, D, dtype=F32)], 4 * proj, "space_mix", 18, 1)(
        q, kv, xv, wo, kvo
    )
    spaced, cot = lax.optimization_barrier((spaced, cot))

    tx = lax.all_to_all(spaced.reshape(64, 2, 3 * D), ("chip", "frame"), 0, 0, tiled=True).reshape(n, D)
    tout, tgrad = call(
        time_body,
        (sds((320, D)), sds((n, D))),
        [vmem(320, D), vmem(320, t), vmem(t, 320), w, w, w, w]
        + [trow] * 4 + [tacc] * 4 + [vmem(t, t, dtype=F32), trow],
        10 * proj,
        "time",
        TIME_LIMIT,
        7,
    )(tx, cot.reshape(320, D), perm, permt, tq, tk, tv, to)
    g = lax.all_to_all(tgrad.reshape(64, 2, 3 * D), ("chip", "frame"), 0, 0, tiled=True).reshape(n, D)
    tout = lax.all_to_all(tout.reshape(8, 40, D), "frame", 0, 0, tiled=True).reshape(320, D)
    do = call(do_body, hbm(n, D), [row, w], 2 * proj, "space_do", 14, 2)(g, so)
    do, tout = lax.optimization_barrier((do, tout))
    block = call(perm_body, sds((t, D)), [], proj // 2, "out_unpack", 6)(permt, tout)

    dq, dkv, dkvo, gf, qf, kvf, xf, rqf, rkf, wq, wk, wv = call(
        back_body,
        (row, pair, pair, row, row, pair, row, norms, norms, w, w, w),
        [pair, row, vmem(n, D, dtype=F32), vmem(2, 2, n, D, dtype=F32)],
        10 * proj,
        "space_back",
        BACK_LIMIT,
        11,
    )(g, q, kv, kvo, do, x, rq, rk, sq, sk, sv)
    got = lax.ppermute(dkvo, "core", swap)
    part = call(final_q_body, vmem(n, D, dtype=F32), [], proj, "space_final_q", 12)(qf, rqf, dq, wq)
    grad = call(final_body, sds((n, D)), [], 2 * proj, "space_final", 16)(xf, gf, kvf, rkf, dkv, part, got, wk, wv)
    grad = lax.all_to_all(grad.reshape(8, 48, D), "chip", 0, 0, tiled=True)[:6]
    return block.reshape(6, 48, D), grad


def solution(mesh):
    planes = Mesh(mesh.devices.reshape(8, 8, 2), ("frame", "chip", "core"))
    spec = P("frame", ("chip", "core"), None)
    return jax.shard_map(
        local,
        mesh=planes,
        in_specs=(spec, spec) + (P(),) * 8,
        out_specs=(spec, spec),
        check_vma=False,
    )
```
